512 devices in a mesh: aux: 64 (over z, y_lo, x), kp: 4 (over y_hi), img: 2 (over core).
Axes of the slice: x: 4, y: 8 (y_hi: 4, y_lo: 2; y = y_hi * 2 + y_lo), z: 8, core: 2. Of those that a mesh axis runs over, the one named last changes fastest.
Arguments:
- lattice: int32 [16, 3], P('img'), may hold values from -1 to 1
- kpoints: int32 [8, 3], replicated, may hold values from 0 to 1
- tensors: bfloat16 [16, 4, 4096, 512], P('img', None, 'aux', 'kp'), may hold values from -1.5 to 1.5
- density: bfloat16 [8, 2, 512, 512], P(('kp', 'img'), None, None, 'aux'), may hold values from -0.1875 to 0.1875
Outputs:
- exchange_rows: bfloat16 [8, 2, 4, 4096, 512], P(('kp', 'img'), None, None, 'aux')
- block: float32 [2, 4, 4], replicated
The draws below stay inside these ranges and needn't reach their ends.
All inputs are finite; a program needn't handle non-finite values.
Results may differ from the reference program's by a relative error of at most 0.0063.
Values may be sent and summed in bfloat16 or wider, within the bound.
No kernel may reach another device: no remote copies, remote signals or barrier semaphores. Data moves between devices by JAX's collectives and lax.ppermute only.
A program may use at most 64 MiB of HBM per device.

```python
import math
import jax
import jax.numpy as jnp
from jax import lax

NAO = 512
NAUX = 4096
NK = 8
MESH = 2
ROWS = 4
IMG_DEV = 8
IMAGES = 16
N_IMG = 2


def with_ends(values, rng, least, top_value):
    longest = values.shape.index(max(values.shape))
    spots = []
    for shift in (0, 1):
        where = [jax.random.randint(jax.random.fold_in(rng, axis), (), 0, length) for axis, length in enumerate(values.shape)]
        where[longest] = (where[longest] + shift) % values.shape[longest]
        spots.append(tuple(where))
    return values.at[spots[0]].set(least).at[spots[1]].set(top_value)


def shard_levels(rng, extent, pieces, least, high):
    factor_of, own = 1.0, jax.random.fold_in(rng, 6)
    for dim, shards_of in pieces:
        draws = jnp.exp(jax.random.uniform(jax.random.fold_in(own, dim), (shards_of,), jnp.float32, least / len(pieces), high / len(pieces)))
        factor_of = factor_of * jnp.repeat(draws, extent[dim] // shards_of).reshape([-1 if axis == dim else 1 for axis in range(len(extent))])
    return factor_of


def scatter_about(rng, shape, width, limit, shards=(), held_as=jnp.bfloat16):
    drawn = width * jax.random.normal(rng, shape, jnp.float32)
    if shards:
        drawn = drawn * shard_levels(rng, shape, shards, -0.22, 0.18)
    return jnp.clip(drawn, -limit, limit).astype(held_as)


def setup_inputs(seed: int = 0) -> dict:
    arg_keys = jax.random.split(jax.random.key(seed), 5)
    return {
        "lattice": with_ends(jax.random.randint(arg_keys[0], (IMAGES, 3), -1, 2), jax.random.fold_in(arg_keys[0], 1), -1, 1).astype(jnp.int32),
        "kpoints": with_ends(jax.random.randint(arg_keys[1], (NK, 3), 0, 2), jax.random.fold_in(arg_keys[1], 1), 0, 1).astype(jnp.int32),
        "tensors": scatter_about(arg_keys[2], (IMAGES, ROWS, NAUX, NAO), IMAGES ** -0.5, 1.5, ((0, 2), (2, 64), (3, 4))),
        "density": scatter_about(arg_keys[3], (NK, 2, NAO, NAO), (2 * NAO) ** -0.5, 0.1875, ((0, 8), (3, 64))),
    }


def phase_table(lattice, kpoints):
    turns = lax.optimization_barrier(jnp.sum((2 * kpoints[:, None, :] + 1) * lattice[None, :, :], axis=-1))
    turns = jnp.mod(turns, 2 * MESH).astype(jnp.float32)
    angle = math.pi / MESH * turns
    return jnp.stack([jnp.cos(angle), jnp.sin(angle)], axis=1).astype(jnp.bfloat16)

def reference(lattice, kpoints, tensors, density):
    table = phase_table(lattice, kpoints)
    block_real = jnp.zeros((ROWS, ROWS), jnp.float32)
    block_imag = jnp.zeros((ROWS, ROWS), jnp.float32)
    collected = []
    for kpair in range(NK):
        summed = jnp.zeros((2, ROWS * NAUX * NAO), jnp.float32)
        for group_index in range(N_IMG):
            first = group_index * IMG_DEV
            flat = tensors[first:first + IMG_DEV].reshape(IMG_DEV, -1)
            group_sum = jnp.dot(table[kpair, :, first:first + IMG_DEV], flat, preferred_element_type=jnp.float32)
            summed = summed + group_sum.astype(jnp.bfloat16).astype(jnp.float32)
        fitted = summed.astype(jnp.bfloat16).reshape(2, ROWS * NAUX, NAO)
        stacked = jnp.concatenate([fitted[0], fitted[1]], axis=1)
        dens_real = density[kpair, 0]
        dens_imag = density[kpair, 1]
        w_real = jnp.dot(stacked, jnp.concatenate([dens_real, -dens_imag], axis=0), preferred_element_type=jnp.float32)
        w_imag = jnp.dot(stacked, jnp.concatenate([dens_imag, dens_real], axis=0), preferred_element_type=jnp.float32)
        rows_out = jnp.stack([w_real, w_imag]).astype(jnp.bfloat16)
        collected.append(rows_out.reshape(2, ROWS, NAUX, NAO))
        wide_real = rows_out[0].reshape(ROWS, -1).astype(jnp.float32)
        wide_imag = rows_out[1].reshape(ROWS, -1).astype(jnp.float32)
        fit_real = fitted[0].reshape(ROWS, -1).astype(jnp.float32)
        fit_imag = fitted[1].reshape(ROWS, -1).astype(jnp.float32)
        high = lax.Precision.HIGHEST
        block_real = block_real + jnp.dot(wide_real, fit_real.T, precision=high) + jnp.dot(wide_imag, fit_imag.T, precision=high)
        block_imag = block_imag + jnp.dot(wide_imag, fit_real.T, precision=high) - jnp.dot(wide_real, fit_imag.T, precision=high)
    scale = 1.0 / math.sqrt(NK * NAUX * NAO)
    return (jnp.stack(collected), jnp.stack([block_real, block_imag]) * scale)
```

```python
import math

import jax
import jax.numpy as jnp
import numpy as np
from jax import lax
from jax.experimental import pallas as pl
from jax.experimental.pallas import tpu as pltpu
from jax.sharding import Mesh
from jax.sharding import PartitionSpec as P

NAO = 512
NAUX = 4096
NK = 8
MESH = 2
ROWS = 4
LANES = 128

ANGLE = np.float32(math.pi / MESH)
COS = [float(np.cos(ANGLE * np.float32(t), dtype=np.float32)) for t in range(2 * MESH)]
SIN = [float(np.sin(ANGLE * np.float32(t), dtype=np.float32)) for t in range(2 * MESH)]


def pick(turns, values):
    out = jnp.full(turns.shape, values[0], jnp.float32)
    for t in range(1, 2 * MESH):
        out = jnp.where(turns == t, values[t], out)
    return out.astype(jnp.bfloat16).astype(jnp.float32)


def group_sum_kernel(kpts_ref, lat_ref, x_ref, own_ref, send_ref, table):
    img = lax.axis_index("img")
    images, rows, _ = x_ref.shape
    kp_count = own_ref.shape[0]
    lat = [jnp.broadcast_to(lat_ref[:, a : a + 1], (images, LANES)) for a in range(3)]
    for half in range(2):
        for pair in range(kp_count):
            k = 2 * pair + (img if half == 0 else 1 - img)
            turns = jnp.zeros((images, LANES), jnp.int32)
            for a in range(3):
                turns = turns + (2 * kpts_ref[k, a] + 1) * lat[a]
            turns = jnp.bitwise_and(turns, 2 * MESH - 1)
            table[half, pair, 0] = pick(turns, COS)
            table[half, pair, 1] = pick(turns, SIN)
    step = 32

    def body(t, carry):
        at = pl.ds(pl.multiple_of(t * step, step), step)
        blocks = [x_ref[r, at, :].astype(jnp.float32) for r in range(images)]
        for half, out_ref in enumerate((own_ref, send_ref)):
            for pair in range(kp_count):
                for c in range(2):
                    acc = None
                    for r in range(images):
                        term = table[half, pair, c, r : r + 1, :] * blocks[r]
                        acc = term if acc is None else acc + term
                    out_ref[pair, c, at, :] = acc.astype(jnp.bfloat16)
        return carry

    lax.fori_loop(0, rows // step, body, 0)


def group_sums(kpoints, lattice, x, kp_count):
    images, rows, cols = x.shape
    out = jax.ShapeDtypeStruct((kp_count, 2, rows, cols), jnp.bfloat16)
    vmem = pl.BlockSpec(memory_space=pltpu.VMEM)
    return pl.pallas_call(
        group_sum_kernel,
        out_shape=(out, out),
        in_specs=[pl.BlockSpec(memory_space=pltpu.SMEM), vmem, vmem],
        out_specs=(vmem, vmem),
        scratch_shapes=[pltpu.VMEM((2, kp_count, 2, images, LANES), jnp.float32)],
        compiler_params=pltpu.CompilerParams(vmem_limit_bytes=24 * 1024 * 1024),
        name="group_sums",
    )(kpoints, lattice, x)


def nt(a, b):
    return lax.dot_general(a, b, (((1,), (1,)), ((), ())), preferred_element_type=jnp.float32)


def rows_kernel(f_ref, g_ref, w_ref, part_ref, dens):
    xs, groups, pack, _ = g_ref.shape
    half = pack // 2
    for g in range(groups):
        for x in range(0, xs, 2):
            first, second = g_ref[x, g], g_ref[x + 1, g]
            at = pl.ds((g * xs + x) * half, pack)
            for c in range(2):
                cut = slice(c * half, (c + 1) * half)
                dens[c, at, :] = jnp.concatenate([first[cut], second[cut]], axis=0)
    blocks = f_ref.shape[0]
    f_real = jnp.concatenate([f_ref[b, 0] for b in range(blocks)], axis=1)
    f_imag = jnp.concatenate([f_ref[b, 1] for b in range(blocks)], axis=1)
    d_real, d_imag = dens[0], dens[1]
    w_real = (nt(f_real, d_real) - nt(f_imag, d_imag)).astype(jnp.bfloat16)
    w_imag = (nt(f_real, d_imag) + nt(f_imag, d_real)).astype(jnp.bfloat16)
    w_ref[0] = w_real
    w_ref[1] = w_imag
    n = f_real.shape[0]
    aux = n // ROWS
    row = lax.broadcasted_iota(jnp.int32, (n, n), 0)
    col = lax.broadcasted_iota(jnp.int32, (n, n), 1)
    same = jnp.bitwise_and(row, aux - 1) == jnp.bitwise_and(col, aux - 1)
    sums = []
    for gram in (
        nt(w_real, f_real) + nt(w_imag, f_imag),
        nt(w_imag, f_real) - nt(w_real, f_imag),
    ):
        kept = jnp.where(same, gram, 0.0)
        for i in range(ROWS):
            sums.append(jnp.sum(kept[i * aux : (i + 1) * aux], axis=0, keepdims=True))
    stacked = jnp.concatenate(sums, axis=0)
    count = 2 * ROWS
    lane = lax.broadcasted_iota(jnp.int32, (count, LANES), 1)
    sub = lax.broadcasted_iota(jnp.int32, (count, LANES), 0)
    out = jnp.zeros((count, LANES), jnp.float32)
    at_col = lax.broadcasted_iota(jnp.int32, (count, n), 1)
    for j in range(ROWS):
        mine = jnp.logical_and(at_col >= j * aux, at_col < (j + 1) * aux)
        total = jnp.sum(jnp.where(mine, stacked, 0.0), axis=1, keepdims=True)
        out = out + jnp.where(lane == sub * ROWS + j, total, 0.0)
    part_ref[...] = jnp.sum(out, axis=0, keepdims=True)


def exchange(f, g):
    blocks, _, rows, width = f.shape
    n = blocks * width
    vmem = pl.BlockSpec(memory_space=pltpu.VMEM)
    return pl.pallas_call(
        rows_kernel,
        out_shape=(
            jax.ShapeDtypeStruct((2, rows, n), jnp.bfloat16),
            jax.ShapeDtypeStruct((1, LANES), jnp.float32),
        ),
        in_specs=[vmem, vmem],
        out_specs=(vmem, vmem),
        scratch_shapes=[pltpu.VMEM((2, n, n), jnp.bfloat16)],
        compiler_params=pltpu.CompilerParams(vmem_limit_bytes=32 * 1024 * 1024),
        name="exchange",
    )(f, g)


def sum_over(part, axes):
    count = lax.axis_size(axes)
    spread = jnp.broadcast_to(part[None], (count,) + part.shape)
    return jnp.sum(lax.all_to_all(spread, axes, 0, 0, tiled=True), axis=0)


def on_device(lattice, kpoints, tensors, density):
    kp_count = lax.axis_size("kp")
    images, rows, aux_local, orb_local = tensors.shape
    n = orb_local * kp_count
    near = lax.axis_size(("z", "ylo"))
    piece = density[0].transpose(0, 2, 1).reshape(-1, n)
    spread = jnp.broadcast_to(piece[None], (near,) + piece.shape)
    gathered = lax.all_to_all(spread, ("z", "ylo"), 0, 0, tiled=True)
    gathered, tensors = lax.optimization_barrier((gathered, tensors))
    dens = lax.all_gather(gathered.reshape(-1, n), "x", axis=0)
    dens = dens.reshape(-1, near, piece.shape[0], n)

    own, send = group_sums(kpoints, lattice, tensors.reshape(images, -1, orb_local), kp_count)
    got = lax.ppermute(send, "img", [(0, 1), (1, 0)])
    fitted = (own.astype(jnp.float32) + got.astype(jnp.float32)).astype(jnp.bfloat16)
    fitted = lax.all_to_all(fitted, "kp", 0, 0, tiled=True)

    products, part = exchange(fitted, dens)
    part = lax.psum(part, ("ylo", "img"))
    part = sum_over(part, ("z", "x", "kp"))
    scale = 1.0 / math.sqrt(NK * NAUX * NAO)
    block = part[0, : 2 * ROWS * ROWS].reshape(2, ROWS, ROWS) * scale
    return products.reshape(1, 2, rows, aux_local, n), block


def solution(mesh):
    fine = Mesh(mesh.devices.reshape(8, 2, 4, 4, 2), ("z", "ylo", "x", "kp", "img"))
    aux = ("z", "ylo", "x")
    return jax.shard_map(
        on_device,
        mesh=fine,
        in_specs=(
            P("img", None),
            P(),
            P("img", None, aux, "kp"),
            P(("kp", "img"), None, None, aux),
        ),
        out_specs=(P(("kp", "img"), None, None, aux, None), P()),
        check_vma=False,
    )
```

```python
import functools
import math

import jax
import jax.numpy as jnp
import numpy as np
from jax import lax
from jax.experimental import pallas as pl
from jax.experimental.pallas import tpu as pltpu
from jax.sharding import Mesh
from jax.sharding import PartitionSpec as P

NAO = 512
NAUX = 4096
NK = 8
MESH = 2
ROWS = 4
LANES = 128
PIECES = (3, 3, 2)

ANGLE = np.float32(math.pi / MESH)
COS = [float(np.cos(ANGLE * np.float32(t), dtype=np.float32)) for t in range(2 * MESH)]
SIN = [float(np.sin(ANGLE * np.float32(t), dtype=np.float32)) for t in range(2 * MESH)]


def pick(turns, values):
    out = jnp.full(turns.shape, values[0], jnp.float32)
    for t in range(1, 2 * MESH):
        out = jnp.where(turns == t, values[t], out)
    return out.astype(jnp.bfloat16).astype(jnp.float32)


def group_sum_kernel(kpts_ref, lat_ref, x_ref, own_ref, *refs):
    *send_refs, table = refs
    img = lax.axis_index("img")
    images, rows, _ = x_ref.shape
    kp_count = own_ref.shape[0] // 2
    targets = [
        [(own_ref, m) for m in range(2 * kp_count)],
        [(ref, m) for ref in send_refs for m in range(ref.shape[0])],
    ]
    lat = [jnp.broadcast_to(lat_ref[:, a : a + 1], (images, LANES)) for a in range(3)]
    for half in range(2):
        for pair in range(kp_count):
            k = 2 * pair + (img if half == 0 else 1 - img)
            turns = jnp.zeros((images, LANES), jnp.int32)
            for a in range(3):
                turns = turns + (2 * kpts_ref[k, a] + 1) * lat[a]
            turns = jnp.bitwise_and(turns, 2 * MESH - 1)
            table[half, pair, 0] = pick(turns, COS)
            table[half, pair, 1] = pick(turns, SIN)
    step = 32

    def body(t, carry):
        at = pl.ds(pl.multiple_of(t * step, step), step)
        blocks = [x_ref[r, at, :].astype(jnp.float32) for r in range(images)]
        for half in range(2):
            for m, (out_ref, place) in enumerate(targets[half]):
                acc = None
                for r in range(images):
                    term = table[half, m // 2, m % 2, r : r + 1, :] * blocks[r]
                    acc = term if acc is None else acc + term
                out_ref[place, at, :] = acc.astype(jnp.bfloat16)
        return carry

    lax.fori_loop(0, rows // step, body, 0)


def group_sums(kpoints, lattice, x, kp_count):
    images, rows, cols = x.shape
    outs = [
        jax.ShapeDtypeStruct((m, rows, cols), jnp.bfloat16) for m in (2 * kp_count,) + PIECES
    ]
    vmem = pl.BlockSpec(memory_space=pltpu.VMEM)
    return pl.pallas_call(
        group_sum_kernel,
        out_shape=outs,
        in_specs=[pl.BlockSpec(memory_space=pltpu.SMEM), vmem, vmem],
        out_specs=[vmem] * len(outs),
        scratch_shapes=[pltpu.VMEM((2, kp_count, 2, images, LANES), jnp.float32)],
        compiler_params=pltpu.CompilerParams(vmem_limit_bytes=24 * 1024 * 1024),
        name="group_sums",
    )(kpoints, lattice, x)


def nt(a, b):
    return lax.dot_general(a, b, (((1,), (1,)), ((), ())), preferred_element_type=jnp.float32)


def rows_kernel(f_ref, g0_ref, g1_ref, g2_ref, g3_ref, w_ref, part_ref, dens):
    held = (g0_ref, g1_ref, g2_ref, g3_ref)
    xs = len(held)
    groups, pack, _ = g0_ref.shape
    half = pack // 2
    me = lax.axis_index("x")

    def place(mine):
        for g in range(groups):
            for x in range(0, xs, 2):
                first, second = held[mine ^ x][g], held[mine ^ (x + 1)][g]
                at = pl.ds((g * xs + x) * half, pack)
                for c in range(2):
                    cut = slice(c * half, (c + 1) * half)
                    dens[c, at, :] = jnp.concatenate([first[cut], second[cut]], axis=0)

    for mine in range(xs):
        pl.when(me == mine)(functools.partial(place, mine))
    blocks = f_ref.shape[0]
    f_real = jnp.concatenate([f_ref[b, 0] for b in range(blocks)], axis=1)
    f_imag = jnp.concatenate([f_ref[b, 1] for b in range(blocks)], axis=1)
    d_real, d_imag = dens[0], dens[1]
    w_real = (nt(f_real, d_real) - nt(f_imag, d_imag)).astype(jnp.bfloat16)
    w_imag = (nt(f_real, d_imag) + nt(f_imag, d_real)).astype(jnp.bfloat16)
    w_ref[0] = w_real
    w_ref[1] = w_imag
    n = f_real.shape[0]
    aux = n // ROWS
    row = lax.broadcasted_iota(jnp.int32, (n, n), 0)
    col = lax.broadcasted_iota(jnp.int32, (n, n), 1)
    same = jnp.bitwise_and(row, aux - 1) == jnp.bitwise_and(col, aux - 1)
    sums = []
    for gram in (
        nt(w_real, f_real) + nt(w_imag, f_imag),
        nt(w_imag, f_real) - nt(w_real, f_imag),
    ):
        kept = jnp.where(same, gram, 0.0)
        for i in range(ROWS):
            sums.append(jnp.sum(kept[i * aux : (i + 1) * aux], axis=0, keepdims=True))
    stacked = jnp.concatenate(sums, axis=0)
    count = 2 * ROWS
    lane = lax.broadcasted_iota(jnp.int32, (count, LANES), 1)
    sub = lax.broadcasted_iota(jnp.int32, (count, LANES), 0)
    out = jnp.zeros((count, LANES), jnp.float32)
    at_col = lax.broadcasted_iota(jnp.int32, (count, n), 1)
    for j in range(ROWS):
        mine = jnp.logical_and(at_col >= j * aux, at_col < (j + 1) * aux)
        total = jnp.sum(jnp.where(mine, stacked, 0.0), axis=1, keepdims=True)
        out = out + jnp.where(lane == sub * ROWS + j, total, 0.0)
    part_ref[...] = jnp.sum(out, axis=0, keepdims=True)


def exchange(f, held):
    blocks, _, rows, width = f.shape
    n = blocks * width
    vmem = pl.BlockSpec(memory_space=pltpu.VMEM)
    return pl.pallas_call(
        rows_kernel,
        out_shape=(
            jax.ShapeDtypeStruct((2, rows, n), jnp.bfloat16),
            jax.ShapeDtypeStruct((1, LANES), jnp.float32),
        ),
        in_specs=[vmem] * (1 + len(held)),
        out_specs=(vmem, vmem),
        scratch_shapes=[pltpu.VMEM((2, n, n), jnp.bfloat16)],
        compiler_params=pltpu.CompilerParams(vmem_limit_bytes=32 * 1024 * 1024),
        name="exchange",
    )(f, *held)


def sum_over(part, axes):
    count = lax.axis_size(axes)
    spread = jnp.broadcast_to(part[None], (count,) + part.shape)
    return jnp.sum(lax.all_to_all(spread, axes, 0, 0, tiled=True), axis=0)


def on_device(lattice, kpoints, tensors, density):
    kp_count = lax.axis_size("kp")
    images, rows, aux_local, orb_local = tensors.shape
    n = orb_local * kp_count
    near = lax.axis_size(("z", "ylo"))
    piece = density[0].transpose(0, 2, 1).reshape(-1, n)
    spread = jnp.broadcast_to(piece[None], (near,) + piece.shape)
    spread, tensors, kpoints, lattice = lax.optimization_barrier((spread, tensors, kpoints, lattice))
    gathered = lax.all_to_all(spread, ("z", "ylo"), 0, 0, tiled=True)
    xs = lax.axis_size("x")
    held = [gathered] + [
        lax.ppermute(gathered, "x", [(i, i ^ step) for i in range(xs)]) for step in range(1, xs)
    ]

    own, *send = group_sums(kpoints, lattice, tensors.reshape(images, -1, orb_local), kp_count)
    got = [lax.ppermute(part, "img", [(0, 1), (1, 0)]) for part in send]
    got = jnp.concatenate(got, axis=0)
    fitted = (own.astype(jnp.float32) + got.astype(jnp.float32)).astype(jnp.bfloat16)
    fitted = fitted.reshape((kp_count, 2) + fitted.shape[1:])
    fitted = lax.all_to_all(fitted, "kp", 0, 0, tiled=True)

    products, part = exchange(fitted, held)
    part = sum_over(part, ("z", "img"))
    part = sum_over(part, ("x", "ylo", "kp"))
    scale = 1.0 / math.sqrt(NK * NAUX * NAO)
    block = part[0, : 2 * ROWS * ROWS].reshape(2, ROWS, ROWS) * scale
    return products.reshape(1, 2, rows, aux_local, n), block


def solution(mesh):
    fine = Mesh(mesh.devices.reshape(8, 2, 4, 4, 2), ("z", "ylo", "x", "kp", "img"))
    aux = ("z", "ylo", "x")
    return jax.shard_map(
        on_device,
        mesh=fine,
        in_specs=(
            P("img", None),
            P(),
            P("img", None, aux, "kp"),
            P(("kp", "img"), None, None, aux),
        ),
        out_specs=(P(("kp", "img"), None, None, aux, None), P()),
        check_vma=False,
    )
```

```python
import math

import jax
import jax.numpy as jnp
import numpy as np
from jax import lax
from jax.experimental import pallas as pl
from jax.experimental.pallas import tpu as pltpu
from jax.sharding import Mesh
from jax.sharding import PartitionSpec as P

NAO = 512
NAUX = 4096
NK = 8
MESH = 2
ROWS = 4
LANES = 128
PIECES = (4,)
JOIN_COST = 30_000_000_000

ANGLE = np.float32(math.pi / MESH)
COS = [float(np.cos(ANGLE * np.float32(t), dtype=np.float32)) for t in range(2 * MESH)]
SIN = [float(np.sin(ANGLE * np.float32(t), dtype=np.float32)) for t in range(2 * MESH)]
SMEM = pl.BlockSpec(memory_space=pltpu.SMEM)
VMEM = pl.BlockSpec(memory_space=pltpu.VMEM)


def pick(turns, values):
    out = jnp.full(turns.shape, values[0], jnp.float32)
    for t in range(1, 2 * MESH):
        out = jnp.where(turns == t, values[t], out)
    return out.astype(jnp.bfloat16).astype(jnp.float32)


def group_sum_kernel(kpts_ref, lat_ref, x_ref, own_ref, *refs):
    *send_refs, table = refs
    img, kp = lax.axis_index("img"), lax.axis_index("kp")
    images, rows, _ = x_ref.shape
    kp_count = own_ref.shape[0]
    targets = [
        [(own_ref, j) for j in range(kp_count)],
        [(ref, j) for ref in send_refs for j in range(ref.shape[0])],
    ]
    sub = lax.broadcasted_iota(jnp.int32, (images, LANES), 0)
    lat = []
    for a in range(3):
        column = jnp.zeros((images, LANES), jnp.int32)
        for r in range(images):
            column = jnp.where(sub == r, lat_ref[a, r], column)
        lat.append(column)
    for half in range(2):
        for j in range(kp_count):
            k = 2 * jnp.bitwise_xor(kp, j) + (img if half == 0 else 1 - img)
            turns = jnp.zeros((images, LANES), jnp.int32)
            for a in range(3):
                turns = turns + (2 * kpts_ref[a, k] + 1) * lat[a]
            turns = jnp.bitwise_and(turns, 2 * MESH - 1)
            table[half, j, 0] = pick(turns, COS)
            table[half, j, 1] = pick(turns, SIN)
    step = 32

    def body(t, carry):
        at = pl.ds(pl.multiple_of(t * step, step), step)
        blocks = [x_ref[r, at, :].astype(jnp.float32) for r in range(images)]
        for half in range(2):
            for j, (out_ref, place) in enumerate(targets[half]):
                for c in range(2):
                    acc = None
                    for r in range(images):
                        term = table[half, j, c, r : r + 1, :] * blocks[r]
                        acc = term if acc is None else acc + term
                    out_ref[place, c, at, :] = acc.astype(jnp.bfloat16)
        return carry

    lax.fori_loop(0, rows // step, body, 0)


def group_sums(kpoints, lattice, x, kp_count):
    images, rows, cols = x.shape
    outs = [
        jax.ShapeDtypeStruct((m, 2, rows, cols), jnp.bfloat16) for m in (kp_count,) + PIECES
    ]
    return pl.pallas_call(
        group_sum_kernel,
        out_shape=outs,
        in_specs=[SMEM, SMEM, VMEM],
        out_specs=[VMEM] * len(outs),
        scratch_shapes=[pltpu.VMEM((2, kp_count, 2, images, LANES), jnp.float32)],
        compiler_params=pltpu.CompilerParams(vmem_limit_bytes=24 * 1024 * 1024),
        name="group_sums",
    )(kpoints.T, lattice.T, x)


def add_groups_kernel(own_ref, *refs):
    count = own_ref.shape[0]
    got, outs = refs[:-count], refs[-count:]
    blocks = [ref.at[j] for ref in got for j in range(ref.shape[0])]
    for j in range(count):
        total = own_ref[j].astype(jnp.float32) + blocks[j][...].astype(jnp.float32)
        outs[j][...] = total.astype(jnp.bfloat16)


def add_groups(own, got):
    return pl.pallas_call(
        add_groups_kernel,
        out_shape=[jax.ShapeDtypeStruct(own.shape[1:], own.dtype)] * own.shape[0],
        in_specs=[VMEM] * (1 + len(got)),
        out_specs=[VMEM] * own.shape[0],
        compiler_params=pltpu.CompilerParams(vmem_limit_bytes=16 * 1024 * 1024),
        name="add_groups",
    )(own, *got)


def spread_kernel(x_ref, o_ref):
    for i in range(o_ref.shape[0]):
        o_ref[i] = x_ref[...]


def spread(x, count):
    return pl.pallas_call(
        spread_kernel,
        out_shape=jax.ShapeDtypeStruct((count,) + x.shape, x.dtype),
        in_specs=[VMEM],
        out_specs=VMEM,
        compiler_params=pltpu.CompilerParams(vmem_limit_bytes=16 * 1024 * 1024),
        name="spread",
    )(x)


def nt(a, b):
    return lax.dot_general(a, b, (((1,), (1,)), ((), ())), preferred_element_type=jnp.float32)


def join_kernel(f0_ref, f1_ref, f2_ref, f3_ref, fit_ref):
    kp = lax.axis_index("kp")
    width = f0_ref.shape[2]
    for j, ref in enumerate((f0_ref, f1_ref, f2_ref, f3_ref)):
        at = pl.ds(pl.multiple_of(jnp.bitwise_xor(kp, j) * width, width), width)
        for c in range(2):
            fit_ref[c, :, at] = ref[c]


def join(fitted):
    _, rows, width = fitted[0].shape
    out = jax.ShapeDtypeStruct((2, rows, width * len(fitted)), jnp.bfloat16)
    return pl.pallas_call(
        join_kernel,
        out_shape=out,
        in_specs=[VMEM] * len(fitted),
        out_specs=VMEM,
        compiler_params=pltpu.CompilerParams(vmem_limit_bytes=16 * 1024 * 1024),
        cost_estimate=pl.CostEstimate(
            flops=JOIN_COST, bytes_accessed=2 * out.size * 2, transcendentals=0
        ),
        name="join",
    )(*fitted)


def rows_kernel(fit_ref, g_ref, w_ref, part_ref, dens):
    xs, groups, pack, _ = g_ref.shape
    half = pack // 2
    for g in range(groups):
        for x in range(0, xs, 2):
            first, second = g_ref[x, g], g_ref[x + 1, g]
            at = pl.ds((g * xs + x) * half, pack)
            for c in range(2):
                cut = slice(c * half, (c + 1) * half)
                dens[c, at, :] = jnp.concatenate([first[cut], second[cut]], axis=0)
    f_real, f_imag = fit_ref[0], fit_ref[1]
    d_real, d_imag = dens[0], dens[1]
    w_real = (nt(f_real, d_real) - nt(f_imag, d_imag)).astype(jnp.bfloat16)
    w_imag = (nt(f_real, d_imag) + nt(f_imag, d_real)).astype(jnp.bfloat16)
    w_ref[0] = w_real
    w_ref[1] = w_imag
    n = f_real.shape[0]
    aux = n // ROWS
    row = lax.broadcasted_iota(jnp.int32, (n, n), 0)
    col = lax.broadcasted_iota(jnp.int32, (n, n), 1)
    same = jnp.bitwise_and(row, aux - 1) == jnp.bitwise_and(col, aux - 1)
    sums = []
    for gram in (
        nt(w_real, f_real) + nt(w_imag, f_imag),
        nt(w_imag, f_real) - nt(w_real, f_imag),
    ):
        kept = jnp.where(same, gram, 0.0)
        for i in range(ROWS):
            sums.append(jnp.sum(kept[i * aux : (i + 1) * aux], axis=0, keepdims=True))
    stacked = jnp.concatenate(sums, axis=0)
    count = 2 * ROWS
    lane = lax.broadcasted_iota(jnp.int32, (count, LANES), 1)
    sub = lax.broadcasted_iota(jnp.int32, (count, LANES), 0)
    out = jnp.zeros((count, LANES), jnp.float32)
    at_col = lax.broadcasted_iota(jnp.int32, (count, n), 1)
    for j in range(ROWS):
        mine = jnp.logical_and(at_col >= j * aux, at_col < (j + 1) * aux)
        total = jnp.sum(jnp.where(mine, stacked, 0.0), axis=1, keepdims=True)
        out = out + jnp.where(lane == sub * ROWS + j, total, 0.0)
    part_ref[...] = jnp.sum(out, axis=0, keepdims=True)


def exchange(fitted, g):
    _, rows, n = fitted.shape
    return pl.pallas_call(
        rows_kernel,
        out_shape=(
            jax.ShapeDtypeStruct((2, rows, n), jnp.bfloat16),
            jax.ShapeDtypeStruct((1, LANES), jnp.float32),
        ),
        in_specs=[VMEM, VMEM],
        out_specs=(VMEM, VMEM),
        scratch_shapes=[pltpu.VMEM((2, n, n), jnp.bfloat16)],
        compiler_params=pltpu.CompilerParams(vmem_limit_bytes=32 * 1024 * 1024),
        name="exchange",
    )(fitted, g)


def sum_over(part, axes):
    count = lax.axis_size(axes)
    block = jnp.broadcast_to(part[None], (count,) + part.shape)
    return jnp.sum(lax.all_to_all(block, axes, 0, 0, tiled=True), axis=0)


def on_device(lattice, kpoints, tensors, density):
    kp_count = lax.axis_size("kp")
    images, rows, aux_local, orb_local = tensors.shape
    n = orb_local * kp_count
    near, xs = lax.axis_size(("z", "ylo")), lax.axis_size("x")
    piece = density[0].transpose(0, 2, 1).reshape(-1, n)
    block = spread(piece, near)
    dens = lax.all_to_all(block, ("z", "ylo"), 0, 0, tiled=True)
    dens = lax.all_to_all(spread(dens, xs), "x", 0, 0, tiled=True)

    own, *send = group_sums(kpoints, lattice, tensors.reshape(images, -1, orb_local), kp_count)
    got = [lax.ppermute(part, "img", [(0, 1), (1, 0)]) for part in send]
    fitted = add_groups(own, got)
    fitted = [
        block if j == 0 else lax.ppermute(block, "kp", [(i, i ^ j) for i in range(kp_count)])
        for j, block in enumerate(fitted)
    ]

    products, part = exchange(join(fitted), dens)
    part = sum_over(part, ("z", "img"))
    part = sum_over(part, ("x", "ylo", "kp"))
    scale = 1.0 / math.sqrt(NK * NAUX * NAO)
    tile = part[0, : 2 * ROWS * ROWS].reshape(2, ROWS, ROWS) * scale
    return products.reshape(1, 2, rows, aux_local, n), tile


def solution(mesh):
    fine = Mesh(mesh.devices.reshape(8, 2, 4, 4, 2), ("z", "ylo", "x", "kp", "img"))
    aux = ("z", "ylo", "x")
    return jax.shard_map(
        on_device,
        mesh=fine,
        in_specs=(
            P("img", None),
            P(),
            P("img", None, aux, "kp"),
            P(("kp", "img"), None, None, aux),
        ),
        out_specs=(P(("kp", "img"), None, None, aux, None), P()),
        check_vma=False,
    )
```

```python
import math

import jax
import jax.numpy as jnp
import numpy as np
from jax import lax
from jax.experimental import pallas as pl
from jax.experimental.pallas import tpu as pltpu
from jax.sharding import Mesh
from jax.sharding import PartitionSpec as P

NAO = 512
NAUX = 4096
NK = 8
MESH = 2
ROWS = 4
LANES = 128
JOIN_COST = 30_000_000_000

ANGLE = np.float32(math.pi / MESH)
COS = [float(np.cos(ANGLE * np.float32(t), dtype=np.float32)) for t in range(2 * MESH)]
SIN = [float(np.sin(ANGLE * np.float32(t), dtype=np.float32)) for t in range(2 * MESH)]
HBM = pl.BlockSpec(memory_space=pltpu.HBM)
VMEM = pl.BlockSpec(memory_space=pltpu.VMEM)


def pick(turns, values):
    out = jnp.full(turns.shape, values[0], jnp.float32)
    for t in range(1, 2 * MESH):
        out = jnp.where(turns == t, values[t], out)
    return out.astype(jnp.bfloat16).astype(jnp.float32)


STEP = 32


def group_sum_kernel(
    kpts_hbm, lat_hbm, x_hbm, dens_hbm, own_hbm, send_hbm, spread_hbm, table,
    kpts_ref, lat_ref, x_ref, dens_ref, own_ref, send_ref, small_sems, x_sems, out_sems, spread_sems,
):
    img, kp = lax.axis_index("img"), lax.axis_index("kp")
    images, rows, _ = x_ref.shape
    kp_count = own_ref.shape[0]
    small = [
        pltpu.make_async_copy(src, dst, small_sems.at[i])
        for i, (src, dst) in enumerate(
            ((kpts_hbm, kpts_ref), (lat_hbm, lat_ref), (dens_hbm, dens_ref))
        )
    ]

    def block_copy(t):
        at = pl.ds(pl.multiple_of(t * STEP, STEP), STEP)
        return pltpu.make_async_copy(x_hbm.at[:, at], x_ref.at[:, at], x_sems.at[t])

    def out_copies(t):
        at = pl.ds(pl.multiple_of(t * STEP, STEP), STEP)
        return [
            pltpu.make_async_copy(ref.at[:, :, at], hbm.at[:, :, at], out_sems.at[half, t])
            for half, (ref, hbm) in enumerate(((own_ref, own_hbm), (send_ref, send_hbm)))
        ]

    def spread_copy(i):
        return pltpu.make_async_copy(dens_ref, spread_hbm.at[i], spread_sems.at[i])

    for copy in small:
        copy.start()
    for t in range(rows // STEP):
        block_copy(t).start()
    small[0].wait()
    small[1].wait()
    sub = lax.broadcasted_iota(jnp.int32, (images, LANES), 0)
    lat = []
    for a in range(3):
        column = jnp.zeros((images, LANES), jnp.int32)
        for r in range(images):
            column = jnp.where(sub == r, lat_ref[a, r], column)
        lat.append(column)
    for half in range(2):
        for j in range(kp_count):
            k = 2 * jnp.bitwise_xor(kp, j) + (img if half == 0 else 1 - img)
            turns = jnp.zeros((images, LANES), jnp.int32)
            for a in range(3):
                turns = turns + (2 * kpts_ref[a, k] + 1) * lat[a]
            turns = jnp.bitwise_and(turns, 2 * MESH - 1)
            table[half, j, 0] = pick(turns, COS)
            table[half, j, 1] = pick(turns, SIN)
    small[2].wait()
    for i in range(spread_hbm.shape[0]):
        spread_copy(i).start()

    def body(t, carry):
        block_copy(t).wait()
        at = pl.ds(pl.multiple_of(t * STEP, STEP), STEP)
        blocks = [x_ref[r, at, :].astype(jnp.float32) for r in range(images)]
        for half, out_ref in enumerate((own_ref, send_ref)):
            for j in range(kp_count):
                for c in range(2):
                    acc = None
                    for r in range(images):
                        term = table[half, j, c, r : r + 1, :] * blocks[r]
                        acc = term if acc is None else acc + term
                    out_ref[j, c, at, :] = acc.astype(jnp.bfloat16)
        for copy in out_copies(t):
            copy.start()
        return carry

    lax.fori_loop(0, rows // STEP, body, 0)
    for t in range(rows // STEP):
        for copy in out_copies(t):
            copy.wait()
    for i in range(spread_hbm.shape[0]):
        spread_copy(i).wait()


def group_sums(kpoints, lattice, x, piece, kp_count, near):
    images, rows, cols = x.shape
    out = jax.ShapeDtypeStruct((kp_count, 2, rows, cols), jnp.bfloat16)
    return pl.pallas_call(
        group_sum_kernel,
        out_shape=(out, out, jax.ShapeDtypeStruct((near,) + piece.shape, piece.dtype)),
        in_specs=[HBM] * 4,
        out_specs=(HBM, HBM, HBM),
        scratch_shapes=[
            pltpu.VMEM((2, kp_count, 2, images, LANES), jnp.float32),
            pltpu.SMEM(kpoints.shape[::-1], jnp.int32),
            pltpu.SMEM(lattice.shape[::-1], jnp.int32),
            pltpu.VMEM(x.shape, x.dtype),
            pltpu.VMEM(piece.shape, piece.dtype),
            pltpu.VMEM(out.shape, out.dtype),
            pltpu.VMEM(out.shape, out.dtype),
            pltpu.SemaphoreType.DMA((3,)),
            pltpu.SemaphoreType.DMA((rows // STEP,)),
            pltpu.SemaphoreType.DMA((2, rows // STEP)),
            pltpu.SemaphoreType.DMA((near,)),
        ],
        compiler_params=pltpu.CompilerParams(vmem_limit_bytes=56 * 1024 * 1024),
        name="group_sums",
    )(kpoints.T, lattice.T, x, piece)


def add_groups_kernel(own_ref, got_ref, *outs):
    for j, out in enumerate(outs):
        total = own_ref[j].astype(jnp.float32) + got_ref[j].astype(jnp.float32)
        out[...] = total.astype(jnp.bfloat16)


def add_groups(own, got):
    return pl.pallas_call(
        add_groups_kernel,
        out_shape=[jax.ShapeDtypeStruct(own.shape[1:], own.dtype)] * own.shape[0],
        in_specs=[VMEM, VMEM],
        out_specs=[VMEM] * own.shape[0],
        compiler_params=pltpu.CompilerParams(vmem_limit_bytes=16 * 1024 * 1024),
        name="add_groups",
    )(own, got)


def spread_kernel(x_ref, o_hbm, sems):
    copies = [
        pltpu.make_async_copy(x_ref, o_hbm.at[i], sems.at[i]) for i in range(o_hbm.shape[0])
    ]
    for copy in copies:
        copy.start()
    for copy in copies:
        copy.wait()


def spread(x, count):
    return pl.pallas_call(
        spread_kernel,
        out_shape=jax.ShapeDtypeStruct((count,) + x.shape, x.dtype),
        in_specs=[VMEM],
        out_specs=HBM,
        scratch_shapes=[pltpu.SemaphoreType.DMA((count,))],
        compiler_params=pltpu.CompilerParams(vmem_limit_bytes=16 * 1024 * 1024),
        name="spread",
    )(x)


def nt(a, b):
    return lax.dot_general(a, b, (((1,), (1,)), ((), ())), preferred_element_type=jnp.float32)


def join_kernel(*refs):
    out_ref = refs[-1]
    for j, ref in enumerate(refs[:-1]):
        out_ref[j] = ref[...]


def join(blocks):
    out = jax.ShapeDtypeStruct((len(blocks),) + blocks[0].shape, jnp.bfloat16)
    return pl.pallas_call(
        join_kernel,
        out_shape=out,
        in_specs=[VMEM] * len(blocks),
        out_specs=VMEM,
        compiler_params=pltpu.CompilerParams(vmem_limit_bytes=16 * 1024 * 1024),
        cost_estimate=pl.CostEstimate(
            flops=JOIN_COST, bytes_accessed=2 * out.size * 2, transcendentals=0
        ),
        name="join",
    )(*blocks)


def rows_kernel(first_ref, last_ref, g_ref, w_hbm, part_ref, dens, fit, w_ref, sems):
    xs, groups, pack, _ = g_ref.shape
    half = pack // 2
    kp = lax.axis_index("kp")
    width = last_ref.shape[2]
    early = first_ref.shape[0]
    for j in range(early + 1):
        ref = first_ref.at[j] if j < early else last_ref
        at = pl.ds(pl.multiple_of(jnp.bitwise_xor(kp, j) * width, width), width)
        for c in range(2):
            fit[c, :, at] = ref[c]
    for g in range(groups):
        for x in range(0, xs, 2):
            first, second = g_ref[x, g], g_ref[x + 1, g]
            at = pl.ds((g * xs + x) * half, pack)
            for c in range(2):
                cut = slice(c * half, (c + 1) * half)
                dens[c, at, :] = jnp.concatenate([first[cut], second[cut]], axis=0)
    f_real, f_imag = fit[0], fit[1]
    d_real, d_imag = dens[0], dens[1]
    out = [pltpu.make_async_copy(w_ref.at[c], w_hbm.at[c], sems.at[c]) for c in range(2)]
    w_real = (nt(f_real, d_real) - nt(f_imag, d_imag)).astype(jnp.bfloat16)
    w_ref[0] = w_real
    out[0].start()
    w_imag = (nt(f_real, d_imag) + nt(f_imag, d_real)).astype(jnp.bfloat16)
    w_ref[1] = w_imag
    out[1].start()
    n = f_real.shape[0]
    aux = n // ROWS
    row = lax.broadcasted_iota(jnp.int32, (n, n), 0)
    col = lax.broadcasted_iota(jnp.int32, (n, n), 1)
    same = jnp.bitwise_and(row, aux - 1) == jnp.bitwise_and(col, aux - 1)
    sums = []
    for gram in (
        nt(w_real, f_real) + nt(w_imag, f_imag),
        nt(w_imag, f_real) - nt(w_real, f_imag),
    ):
        kept = jnp.where(same, gram, 0.0)
        for i in range(ROWS):
            sums.append(jnp.sum(kept[i * aux : (i + 1) * aux], axis=0, keepdims=True))
    stacked = jnp.concatenate(sums, axis=0)
    count = 2 * ROWS
    lane = lax.broadcasted_iota(jnp.int32, (count, LANES), 1)
    sub = lax.broadcasted_iota(jnp.int32, (count, LANES), 0)
    terms = jnp.zeros((count, LANES), jnp.float32)
    at_col = lax.broadcasted_iota(jnp.int32, (count, n), 1)
    for j in range(ROWS):
        mine = jnp.logical_and(at_col >= j * aux, at_col < (j + 1) * aux)
        total = jnp.sum(jnp.where(mine, stacked, 0.0), axis=1, keepdims=True)
        terms = terms + jnp.where(lane == sub * ROWS + j, total, 0.0)
    part_ref[...] = jnp.sum(terms, axis=0, keepdims=True)
    out[0].wait()
    out[1].wait()


def exchange(first, last, g):
    _, rows, width = last.shape
    n = width * (first.shape[0] + 1)
    wide = jax.ShapeDtypeStruct((2, rows, n), jnp.bfloat16)
    return pl.pallas_call(
        rows_kernel,
        out_shape=(wide, jax.ShapeDtypeStruct((1, LANES), jnp.float32)),
        in_specs=[VMEM] * 3,
        out_specs=(HBM, VMEM),
        scratch_shapes=[
            pltpu.VMEM((2, n, n), jnp.bfloat16),
            pltpu.VMEM(wide.shape, wide.dtype),
            pltpu.VMEM(wide.shape, wide.dtype),
            pltpu.SemaphoreType.DMA((2,)),
        ],
        compiler_params=pltpu.CompilerParams(vmem_limit_bytes=32 * 1024 * 1024),
        name="exchange",
    )(first, last, g)


def tile_kernel(terms_ref, tile_ref):
    total = jnp.sum(terms_ref[:, 0, :], axis=0, keepdims=True)
    count = 2 * ROWS
    lane = lax.broadcasted_iota(jnp.int32, (count, LANES), 1)
    sub = lax.broadcasted_iota(jnp.int32, (count, LANES), 0)
    tile = jnp.zeros((count, LANES), jnp.float32)
    for j in range(ROWS):
        mine = jnp.where(lane == sub * ROWS + j, total, 0.0)
        tile = tile + jnp.where(lane == j, jnp.sum(mine, axis=1, keepdims=True), 0.0)
    tile = tile * (1.0 / math.sqrt(NK * NAUX * NAO))
    for c in range(2):
        tile_ref[c] = tile[c * ROWS : (c + 1) * ROWS, :ROWS]


def tile_of(terms):
    return pl.pallas_call(
        tile_kernel,
        out_shape=jax.ShapeDtypeStruct((2, ROWS, ROWS), jnp.float32),
        in_specs=[VMEM],
        out_specs=VMEM,
        name="tile",
    )(terms)


def terms_over(part, axes):
    count = lax.axis_size(axes)
    block = jnp.broadcast_to(part[None], (count,) + part.shape)
    return lax.all_to_all(block, axes, 0, 0, tiled=True)


def on_device(lattice, kpoints, tensors, density):
    kp_count = lax.axis_size("kp")
    images, rows, aux_local, orb_local = tensors.shape
    n = orb_local * kp_count
    near, xs = lax.axis_size(("z", "ylo")), lax.axis_size("x")
    piece = density[0].transpose(0, 2, 1).reshape(-1, n)
    own, send, block = group_sums(
        kpoints, lattice, tensors.reshape(images, -1, orb_local), piece, kp_count, near
    )
    got = lax.ppermute(send, "img", [(0, 1), (1, 0)])
    dens = lax.all_to_all(block, ("z", "ylo"), 0, 0, tiled=True)
    fitted = add_groups(own, got)
    fitted = [
        block if j == 0 else lax.ppermute(block, "kp", [(i, i ^ j) for i in range(kp_count)])
        for j, block in enumerate(fitted)
    ]
    dens = lax.all_to_all(spread(dens, xs), "x", 0, 0, tiled=True)

    products, part = exchange(join(fitted[:-1]), fitted[-1], dens)
    part = jnp.sum(terms_over(part, ("z", "img")), axis=0)
    tile = tile_of(terms_over(part, ("x", "ylo", "kp")))
    return products.reshape(1, 2, rows, aux_local, n), tile


def solution(mesh):
    fine = Mesh(mesh.devices.reshape(8, 2, 4, 4, 2), ("z", "ylo", "x", "kp", "img"))
    aux = ("z", "ylo", "x")
    return jax.shard_map(
        on_device,
        mesh=fine,
        in_specs=(
            P("img", None),
            P(),
            P("img", None, aux, "kp"),
            P(("kp", "img"), None, None, aux),
        ),
        out_specs=(P(("kp", "img"), None, None, aux, None), P()),
        check_vma=False,
    )
```

```python
import math

import jax
import jax.numpy as jnp
import numpy as np
from jax import lax
from jax.experimental import pallas as pl
from jax.experimental.pallas import tpu as pltpu
from jax.sharding import Mesh
from jax.sharding import PartitionSpec as P

NAO = 512
NAUX = 4096
NK = 8
MESH = 2
ROWS = 4
LANES = 128
JOIN_COST = 30_000_000_000

ANGLE = np.float32(math.pi / MESH)
COS = [float(np.cos(ANGLE * np.float32(t), dtype=np.float32)) for t in range(2 * MESH)]
SIN = [float(np.sin(ANGLE * np.float32(t), dtype=np.float32)) for t in range(2 * MESH)]
HBM = pl.BlockSpec(memory_space=pltpu.HBM)
VMEM = pl.BlockSpec(memory_space=pltpu.VMEM)


def pick(turns, values):
    out = jnp.full(turns.shape, values[0], jnp.float32)
    for t in range(1, 2 * MESH):
        out = jnp.where(turns == t, values[t], out)
    return out.astype(jnp.bfloat16).astype(jnp.float32)


STEP = 32


def phase_sums(blocks, table, j, c):
    acc = None
    for r, block in enumerate(blocks):
        term = table[j, c, r : r + 1, :] * block
        acc = term if acc is None else acc + term
    return acc.astype(jnp.bfloat16)


def partner_kernel(
    kpts_hbm, lat_hbm, x_hbm, dens_hbm, send_hbm, spread_hbm, own_table,
    table, kpts_ref, lat_ref, x_ref, dens_ref, send_ref, small_sems, x_sems, out_sems, spread_sems,
):
    img, kp = lax.axis_index("img"), lax.axis_index("kp")
    images, rows, _ = x_ref.shape
    kp_count = send_ref.shape[0]
    small = [
        pltpu.make_async_copy(src, dst, small_sems.at[i])
        for i, (src, dst) in enumerate(
            ((kpts_hbm, kpts_ref), (lat_hbm, lat_ref), (dens_hbm, dens_ref))
        )
    ]

    def block_copy(t):
        at = pl.ds(pl.multiple_of(t * STEP, STEP), STEP)
        return pltpu.make_async_copy(x_hbm.at[:, at], x_ref.at[:, at], x_sems.at[t])

    def out_copy(t):
        at = pl.ds(pl.multiple_of(t * STEP, STEP), STEP)
        return pltpu.make_async_copy(send_ref.at[:, :, at], send_hbm.at[:, :, at], out_sems.at[t])

    def spread_copy(i):
        return pltpu.make_async_copy(dens_ref, spread_hbm.at[i], spread_sems.at[i])

    for copy in small:
        copy.start()
    for t in range(rows // STEP):
        block_copy(t).start()
    small[0].wait()
    small[1].wait()
    sub = lax.broadcasted_iota(jnp.int32, (images, LANES), 0)
    lat = []
    for a in range(3):
        column = jnp.zeros((images, LANES), jnp.int32)
        for r in range(images):
            column = jnp.where(sub == r, lat_ref[a, r], column)
        lat.append(column)
    for core, phases in ((1 - img, table), (img, own_table)):
        for j in range(kp_count):
            k = 2 * jnp.bitwise_xor(kp, j) + core
            turns = jnp.zeros((images, LANES), jnp.int32)
            for a in range(3):
                turns = turns + (2 * kpts_ref[a, k] + 1) * lat[a]
            turns = jnp.bitwise_and(turns, 2 * MESH - 1)
            phases[j, 0] = pick(turns, COS)
            phases[j, 1] = pick(turns, SIN)
    small[2].wait()
    for i in range(spread_hbm.shape[0]):
        spread_copy(i).start()

    def body(t, carry):
        block_copy(t).wait()
        at = pl.ds(pl.multiple_of(t * STEP, STEP), STEP)
        blocks = [x_ref[r, at, :].astype(jnp.float32) for r in range(images)]
        for j in range(kp_count):
            for c in range(2):
                send_ref[j, c, at, :] = phase_sums(blocks, table, j, c)
        out_copy(t).start()
        return carry

    lax.fori_loop(0, rows // STEP, body, 0)
    for t in range(rows // STEP):
        out_copy(t).wait()
    for i in range(spread_hbm.shape[0]):
        spread_copy(i).wait()


def partner_sums(kpoints, lattice, x, piece, kp_count, near):
    images, rows, cols = x.shape
    out = jax.ShapeDtypeStruct((kp_count, 2, rows, cols), jnp.bfloat16)
    table = jax.ShapeDtypeStruct((kp_count, 2, images, LANES), jnp.float32)
    return pl.pallas_call(
        partner_kernel,
        out_shape=(out, jax.ShapeDtypeStruct((near,) + piece.shape, piece.dtype), table),
        in_specs=[HBM] * 4,
        out_specs=(HBM, HBM, VMEM),
        scratch_shapes=[
            pltpu.VMEM(table.shape, table.dtype),
            pltpu.SMEM(kpoints.shape[::-1], jnp.int32),
            pltpu.SMEM(lattice.shape[::-1], jnp.int32),
            pltpu.VMEM(x.shape, x.dtype),
            pltpu.VMEM(piece.shape, piece.dtype),
            pltpu.VMEM(out.shape, out.dtype),
            pltpu.SemaphoreType.DMA((3,)),
            pltpu.SemaphoreType.DMA((rows // STEP,)),
            pltpu.SemaphoreType.DMA((rows // STEP,)),
            pltpu.SemaphoreType.DMA((near,)),
        ],
        compiler_params=pltpu.CompilerParams(vmem_limit_bytes=56 * 1024 * 1024),
        name="partner_sums",
    )(kpoints.T, lattice.T, x, piece)


def fit_kernel(table, x_ref, got_ref, *outs):
    images, rows, _ = x_ref.shape

    def body(t, carry):
        at = pl.ds(pl.multiple_of(t * STEP, STEP), STEP)
        blocks = [x_ref[r, at, :].astype(jnp.float32) for r in range(images)]
        for j, out in enumerate(outs):
            for c in range(2):
                own = phase_sums(blocks, table, j, c)
                total = own.astype(jnp.float32) + got_ref[j, c, at, :].astype(jnp.float32)
                out[c, at, :] = total.astype(jnp.bfloat16)
        return carry

    lax.fori_loop(0, rows // STEP, body, 0)


def fit(table, x, got):
    return pl.pallas_call(
        fit_kernel,
        out_shape=[jax.ShapeDtypeStruct(got.shape[1:], got.dtype)] * got.shape[0],
        in_specs=[VMEM] * 3,
        out_specs=[VMEM] * got.shape[0],
        compiler_params=pltpu.CompilerParams(vmem_limit_bytes=16 * 1024 * 1024),
        name="fit",
    )(table, x, got)


def spread_kernel(x_ref, o_hbm, sems):
    me = lax.axis_index("x")
    count = o_hbm.shape[0]
    copies = [
        pltpu.make_async_copy(x_ref, o_hbm.at[jnp.bitwise_xor(me, i)], sems.at[i])
        for i in range(1, count)
    ]
    for copy in copies:
        copy.start()
    for copy in copies:
        copy.wait()


def spread(x, count):
    return pl.pallas_call(
        spread_kernel,
        out_shape=jax.ShapeDtypeStruct((count,) + x.shape, x.dtype),
        in_specs=[VMEM],
        out_specs=HBM,
        scratch_shapes=[pltpu.SemaphoreType.DMA((count,))],
        compiler_params=pltpu.CompilerParams(vmem_limit_bytes=16 * 1024 * 1024),
        name="spread",
    )(x)


def nt(a, b):
    return lax.dot_general(a, b, (((1,), (1,)), ((), ())), preferred_element_type=jnp.float32)


def join_kernel(*refs):
    out_ref = refs[-1]
    for j, ref in enumerate(refs[:-1]):
        out_ref[j] = ref[...]


def join(blocks):
    out = jax.ShapeDtypeStruct((len(blocks),) + blocks[0].shape, jnp.bfloat16)
    return pl.pallas_call(
        join_kernel,
        out_shape=out,
        in_specs=[VMEM] * len(blocks),
        out_specs=VMEM,
        compiler_params=pltpu.CompilerParams(vmem_limit_bytes=16 * 1024 * 1024),
        cost_estimate=pl.CostEstimate(
            flops=JOIN_COST, bytes_accessed=2 * out.size * 2, transcendentals=0
        ),
        name="join",
    )(*blocks)


def rows_kernel(
    first_ref, last_ref, own_ref, g_ref, w_hbm, part_ref, dens, fit, w_ref, sems
):
    xs, groups, pack, _ = g_ref.shape
    half = pack // 2
    kp = lax.axis_index("kp")
    width = last_ref.shape[2]
    early = first_ref.shape[0]
    for j in range(early + 1):
        ref = first_ref.at[j] if j < early else last_ref
        at = pl.ds(pl.multiple_of(jnp.bitwise_xor(kp, j) * width, width), width)
        for c in range(2):
            fit[c, :, at] = ref[c]
    me = lax.axis_index("x")
    for g in range(groups):
        mine = own_ref[g]
        for x in range(0, xs, 2):
            first = jnp.where(me == x, mine, g_ref[x, g])
            second = jnp.where(me == x + 1, mine, g_ref[x + 1, g])
            at = pl.ds((g * xs + x) * half, pack)
            for c in range(2):
                cut = slice(c * half, (c + 1) * half)
                dens[c, at, :] = jnp.concatenate([first[cut], second[cut]], axis=0)
    f_real, f_imag = fit[0], fit[1]
    d_real, d_imag = dens[0], dens[1]
    out = [pltpu.make_async_copy(w_ref.at[c], w_hbm.at[c], sems.at[c]) for c in range(2)]
    w_real = (nt(f_real, d_real) - nt(f_imag, d_imag)).astype(jnp.bfloat16)
    w_ref[0] = w_real
    out[0].start()
    w_imag = (nt(f_real, d_imag) + nt(f_imag, d_real)).astype(jnp.bfloat16)
    w_ref[1] = w_imag
    out[1].start()
    n = f_real.shape[0]
    aux = n // ROWS
    row = lax.broadcasted_iota(jnp.int32, (n, n), 0)
    col = lax.broadcasted_iota(jnp.int32, (n, n), 1)
    same = jnp.bitwise_and(row, aux - 1) == jnp.bitwise_and(col, aux - 1)
    sums = []
    for gram in (
        nt(w_real, f_real) + nt(w_imag, f_imag),
        nt(w_imag, f_real) - nt(w_real, f_imag),
    ):
        kept = jnp.where(same, gram, 0.0)
        for i in range(ROWS):
            sums.append(jnp.sum(kept[i * aux : (i + 1) * aux], axis=0, keepdims=True))
    stacked = jnp.concatenate(sums, axis=0)
    count = 2 * ROWS
    lane = lax.broadcasted_iota(jnp.int32, (count, LANES), 1)
    sub = lax.broadcasted_iota(jnp.int32, (count, LANES), 0)
    terms = jnp.zeros((count, LANES), jnp.float32)
    at_col = lax.broadcasted_iota(jnp.int32, (count, n), 1)
    for j in range(ROWS):
        mine = jnp.logical_and(at_col >= j * aux, at_col < (j + 1) * aux)
        total = jnp.sum(jnp.where(mine, stacked, 0.0), axis=1, keepdims=True)
        terms = terms + jnp.where(lane == sub * ROWS + j, total, 0.0)
    part_ref[...] = jnp.sum(terms, axis=0, keepdims=True)
    out[0].wait()
    out[1].wait()


def exchange(first, last, own, g):
    _, rows, width = last.shape
    n = width * (first.shape[0] + 1)
    wide = jax.ShapeDtypeStruct((2, rows, n), jnp.bfloat16)
    return pl.pallas_call(
        rows_kernel,
        out_shape=(wide, jax.ShapeDtypeStruct((1, LANES), jnp.float32)),
        in_specs=[VMEM] * 4,
        out_specs=(HBM, VMEM),
        scratch_shapes=[
            pltpu.VMEM((2, n, n), jnp.bfloat16),
            pltpu.VMEM(wide.shape, wide.dtype),
            pltpu.VMEM(wide.shape, wide.dtype),
            pltpu.SemaphoreType.DMA((2,)),
        ],
        compiler_params=pltpu.CompilerParams(vmem_limit_bytes=32 * 1024 * 1024),
        name="exchange",
    )(first, last, own, g)


def terms_over(part, axes):
    count = lax.axis_size(axes)
    block = jnp.broadcast_to(part[None], (count,) + part.shape)
    return lax.all_to_all(block, axes, 0, 0, tiled=True)


def on_device(lattice, kpoints, tensors, density):
    kp_count = lax.axis_size("kp")
    images, rows, aux_local, orb_local = tensors.shape
    n = orb_local * kp_count
    near, xs = lax.axis_size(("z", "ylo")), lax.axis_size("x")
    piece = density[0].transpose(0, 2, 1).reshape(-1, n)
    images_held = tensors.reshape(images, -1, orb_local)
    send, block, table = partner_sums(kpoints, lattice, images_held, piece, kp_count, near)
    got = lax.ppermute(send, "img", [(0, 1), (1, 0)])
    own = lax.all_to_all(block, ("z", "ylo"), 0, 0, tiled=True)
    fitted = fit(table, images_held, got)
    fitted = [
        block if j == 0 else lax.ppermute(block, "kp", [(i, i ^ j) for i in range(kp_count)])
        for j, block in enumerate(fitted)
    ]
    dens = lax.all_to_all(spread(own, xs), "x", 0, 0, tiled=True)

    products, part = exchange(join(fitted[:-1]), fitted[-1], own, dens)
    part = jnp.sum(terms_over(part, ("z", "img")), axis=0)
    part = jnp.sum(terms_over(part, ("x", "ylo", "kp")), axis=0)
    scale = 1.0 / math.sqrt(NK * NAUX * NAO)
    tile = part[0, : 2 * ROWS * ROWS].reshape(2, ROWS, ROWS) * scale
    return products.reshape(1, 2, rows, aux_local, n), tile


def solution(mesh):
    fine = Mesh(mesh.devices.reshape(8, 2, 4, 4, 2), ("z", "ylo", "x", "kp", "img"))
    aux = ("z", "ylo", "x")
    return jax.shard_map(
        on_device,
        mesh=fine,
        in_specs=(
            P("img", None),
            P(),
            P("img", None, aux, "kp"),
            P(("kp", "img"), None, None, aux),
        ),
        out_specs=(P(("kp", "img"), None, None, aux, None), P()),
        check_vma=False,
    )
```

```python
import math

import jax
import jax.numpy as jnp
import numpy as np
from jax import lax
from jax.experimental import pallas as pl
from jax.experimental.pallas import tpu as pltpu
from jax.sharding import Mesh
from jax.sharding import PartitionSpec as P

NAO = 512
NAUX = 4096
NK = 8
MESH = 2
ROWS = 4
LANES = 128
FAR = 2
JOIN_COST = 30_000_000_000

ANGLE = np.float32(math.pi / MESH)
COS = [float(np.cos(ANGLE * np.float32(t), dtype=np.float32)) for t in range(2 * MESH)]
SIN = [float(np.sin(ANGLE * np.float32(t), dtype=np.float32)) for t in range(2 * MESH)]
HBM = pl.BlockSpec(memory_space=pltpu.HBM)
SMEM = pl.BlockSpec(memory_space=pltpu.SMEM)
VMEM = pl.BlockSpec(memory_space=pltpu.VMEM)


def pick(turns, values):
    out = jnp.full(turns.shape, values[0], jnp.float32)
    for t in range(1, 2 * MESH):
        out = jnp.where(turns == t, values[t], out)
    return out.astype(jnp.bfloat16).astype(jnp.float32)


STEP = 32


def phase_sums(blocks, table, j, c):
    acc = None
    for r, block in enumerate(blocks):
        term = table[j, c, r : r + 1, :] * block
        acc = term if acc is None else acc + term
    return acc.astype(jnp.bfloat16)


def fit_kernel(kpts_ref, lat0_ref, lat1_ref, x0_ref, x1_ref, *refs):
    *outs, table = refs
    img, kp = lax.axis_index("img"), lax.axis_index("kp")
    images, rows, _ = x0_ref.shape
    sub = lax.broadcasted_iota(jnp.int32, (images, LANES), 0)
    for group, lat_ref in enumerate((lat0_ref, lat1_ref)):
        lat = []
        for a in range(3):
            column = jnp.zeros((images, LANES), jnp.int32)
            for r in range(images):
                column = jnp.where(sub == r, lat_ref[a, r], column)
            lat.append(column)
        for j in range(len(outs)):
            k = 2 * jnp.bitwise_xor(kp, j) + img
            turns = jnp.zeros((images, LANES), jnp.int32)
            for a in range(3):
                turns = turns + (2 * kpts_ref[a, k] + 1) * lat[a]
            turns = jnp.bitwise_and(turns, 2 * MESH - 1)
            table[group, j, 0] = pick(turns, COS)
            table[group, j, 1] = pick(turns, SIN)

    def body(t, carry):
        at = pl.ds(pl.multiple_of(t * STEP, STEP), STEP)
        total = None
        for group, x_ref in enumerate((x0_ref, x1_ref)):
            blocks = [x_ref[r, at, :].astype(jnp.float32) for r in range(images)]
            sums = [
                phase_sums(blocks, table.at[group], j, c) for j in range(len(outs)) for c in range(2)
            ]
            sums = [term.astype(jnp.float32) for term in sums]
            total = sums if total is None else [p + q for p, q in zip(total, sums)]
        for m, value in enumerate(total):
            outs[m // 2][m % 2, at, :] = value.astype(jnp.bfloat16)
        return carry

    lax.fori_loop(0, rows // STEP, body, 0)


def fit(kpoints, lattices, groups, kp_count):
    images, rows, cols = groups[0].shape
    out = jax.ShapeDtypeStruct((2, rows, cols), jnp.bfloat16)
    return pl.pallas_call(
        fit_kernel,
        out_shape=[out] * kp_count,
        in_specs=[SMEM] * 3 + [VMEM] * 2,
        out_specs=[VMEM] * kp_count,
        scratch_shapes=[pltpu.VMEM((2, kp_count, 2, images, LANES), jnp.float32)],
        compiler_params=pltpu.CompilerParams(vmem_limit_bytes=16 * 1024 * 1024),
        name="fit",
    )(kpoints, *lattices, *groups)


def fan_kernel(x_hbm, o_hbm, x_ref, in_sem, sems):
    read = pltpu.make_async_copy(x_hbm, x_ref, in_sem)
    read.start()
    read.wait()
    copies = [
        pltpu.make_async_copy(x_ref, o_hbm.at[i], sems.at[i]) for i in range(o_hbm.shape[0])
    ]
    for copy in copies:
        copy.start()
    for copy in copies:
        copy.wait()


def fan(x, count):
    return pl.pallas_call(
        fan_kernel,
        out_shape=jax.ShapeDtypeStruct((count,) + x.shape, x.dtype),
        in_specs=[HBM],
        out_specs=HBM,
        scratch_shapes=[
            pltpu.VMEM(x.shape, x.dtype),
            pltpu.SemaphoreType.DMA,
            pltpu.SemaphoreType.DMA((count,)),
        ],
        compiler_params=pltpu.CompilerParams(vmem_limit_bytes=56 * 1024 * 1024),
        name="fan",
    )(x)


def spread_kernel(x_ref, o_hbm, sems):
    me = lax.axis_index("x")
    count = o_hbm.shape[0]
    copies = [
        pltpu.make_async_copy(x_ref, o_hbm.at[jnp.bitwise_xor(me, i)], sems.at[i])
        for i in range(1, count)
    ]
    for copy in copies:
        copy.start()
    for copy in copies:
        copy.wait()


def spread(x, count):
    return pl.pallas_call(
        spread_kernel,
        out_shape=jax.ShapeDtypeStruct((count,) + x.shape, x.dtype),
        in_specs=[VMEM],
        out_specs=HBM,
        scratch_shapes=[pltpu.SemaphoreType.DMA((count,))],
        compiler_params=pltpu.CompilerParams(vmem_limit_bytes=16 * 1024 * 1024),
        name="spread",
    )(x)


def nt(a, b):
    return lax.dot_general(a, b, (((1,), (1,)), ((), ())), preferred_element_type=jnp.float32)


def join_kernel(*refs):
    out_ref = refs[-1]
    for j, ref in enumerate(refs[:-1]):
        out_ref[j] = ref[...]


def join(blocks):
    out = jax.ShapeDtypeStruct((len(blocks),) + blocks[0].shape, jnp.bfloat16)
    return pl.pallas_call(
        join_kernel,
        out_shape=out,
        in_specs=[VMEM] * len(blocks),
        out_specs=VMEM,
        compiler_params=pltpu.CompilerParams(vmem_limit_bytes=16 * 1024 * 1024),
        cost_estimate=pl.CostEstimate(
            flops=JOIN_COST, bytes_accessed=2 * out.size * 2, transcendentals=0
        ),
        name="join",
    )(*blocks)


def rows_kernel(
    first_ref, near_ref, last_ref, own_ref, g_ref, w_hbm, part_ref, dens, fit, w_ref, sems
):
    xs, groups, pack, _ = g_ref.shape
    half = pack // 2
    kp = lax.axis_index("kp")
    width = last_ref.shape[2]
    for j, ref in ((0, first_ref.at[0]), (FAR, first_ref.at[1]), (1, near_ref), (3, last_ref)):
        at = pl.ds(pl.multiple_of(jnp.bitwise_xor(kp, j) * width, width), width)
        for c in range(2):
            fit[c, :, at] = ref[c]
    me = lax.axis_index("x")
    for g in range(groups):
        mine = own_ref[g]
        for x in range(0, xs, 2):
            first = jnp.where(me == x, mine, g_ref[x, g])
            second = jnp.where(me == x + 1, mine, g_ref[x + 1, g])
            at = pl.ds((g * xs + x) * half, pack)
            for c in range(2):
                cut = slice(c * half, (c + 1) * half)
                dens[c, at, :] = jnp.concatenate([first[cut], second[cut]], axis=0)
    f_real, f_imag = fit[0], fit[1]
    d_real, d_imag = dens[0], dens[1]
    out = [pltpu.make_async_copy(w_ref.at[c], w_hbm.at[c], sems.at[c]) for c in range(2)]
    w_real = (nt(f_real, d_real) - nt(f_imag, d_imag)).astype(jnp.bfloat16)
    w_ref[0] = w_real
    out[0].start()
    w_imag = (nt(f_real, d_imag) + nt(f_imag, d_real)).astype(jnp.bfloat16)
    w_ref[1] = w_imag
    out[1].start()
    n = f_real.shape[0]
    aux = n // ROWS
    row = lax.broadcasted_iota(jnp.int32, (n, n), 0)
    col = lax.broadcasted_iota(jnp.int32, (n, n), 1)
    same = jnp.bitwise_and(row, aux - 1) == jnp.bitwise_and(col, aux - 1)
    sums = []
    for gram in (
        nt(w_real, f_real) + nt(w_imag, f_imag),
        nt(w_imag, f_real) - nt(w_real, f_imag),
    ):
        kept = jnp.where(same, gram, 0.0)
        for i in range(ROWS):
            sums.append(jnp.sum(kept[i * aux : (i + 1) * aux], axis=0, keepdims=True))
    stacked = jnp.concatenate(sums, axis=0)
    count = 2 * ROWS
    lane = lax.broadcasted_iota(jnp.int32, (count, LANES), 1)
    sub = lax.broadcasted_iota(jnp.int32, (count, LANES), 0)
    terms = jnp.zeros((count, LANES), jnp.float32)
    at_col = lax.broadcasted_iota(jnp.int32, (count, n), 1)
    for j in range(ROWS):
        mine = jnp.logical_and(at_col >= j * aux, at_col < (j + 1) * aux)
        total = jnp.sum(jnp.where(mine, stacked, 0.0), axis=1, keepdims=True)
        terms = terms + jnp.where(lane == sub * ROWS + j, total, 0.0)
    part_ref[...] = jnp.sum(terms, axis=0, keepdims=True)
    out[0].wait()
    out[1].wait()


def exchange(first, near, last, own, g):
    _, rows, width = last.shape
    n = width * 4
    wide = jax.ShapeDtypeStruct((2, rows, n), jnp.bfloat16)
    return pl.pallas_call(
        rows_kernel,
        out_shape=(wide, jax.ShapeDtypeStruct((1, LANES), jnp.float32)),
        in_specs=[VMEM] * 5,
        out_specs=(HBM, VMEM),
        scratch_shapes=[
            pltpu.VMEM((2, n, n), jnp.bfloat16),
            pltpu.VMEM(wide.shape, wide.dtype),
            pltpu.VMEM(wide.shape, wide.dtype),
            pltpu.SemaphoreType.DMA((2,)),
        ],
        compiler_params=pltpu.CompilerParams(vmem_limit_bytes=32 * 1024 * 1024),
        name="exchange",
    )(first, near, last, own, g)


def terms_over(part, axes):
    count = lax.axis_size(axes)
    block = jnp.broadcast_to(part[None], (count,) + part.shape)
    return lax.all_to_all(block, axes, 0, 0, tiled=True)


def on_device(lattice, kpoints, tensors, density):
    kp_count = lax.axis_size("kp")
    images, rows, aux_local, orb_local = tensors.shape
    n = orb_local * kp_count
    near, xs = lax.axis_size(("z", "ylo")), lax.axis_size("x")
    piece = density[0].transpose(0, 2, 1).reshape(-1, n)
    swap = [(0, 1), (1, 0)]
    held, lattice = tensors.reshape(images, -1, orb_local), lattice.T
    other, other_lattice = lax.ppermute(held, "img", swap), lax.ppermute(lattice, "img", swap)
    own = lax.all_to_all(fan(piece, near), ("z", "ylo"), 0, 0, tiled=True)
    fitted = fit(kpoints.T, (lattice, other_lattice), (held, other), kp_count)
    fitted = [
        block if j == 0 else lax.ppermute(block, "kp", [(i, i ^ j) for i in range(kp_count)])
        for j, block in enumerate(fitted)
    ]
    dens = lax.all_to_all(spread(own, xs), "x", 0, 0, tiled=True)

    products, part = exchange(join([fitted[0], fitted[FAR]]), fitted[1], fitted[3], own, dens)
    part = jnp.sum(terms_over(part, ("z", "img")), axis=0)
    part = jnp.sum(terms_over(part, ("x", "ylo", "kp")), axis=0)
    scale = 1.0 / math.sqrt(NK * NAUX * NAO)
    tile = part[0, : 2 * ROWS * ROWS].reshape(2, ROWS, ROWS) * scale
    return products.reshape(1, 2, rows, aux_local, n), tile


def solution(mesh):
    fine = Mesh(mesh.devices.reshape(8, 2, 4, 4, 2), ("z", "ylo", "x", "kp", "img"))
    aux = ("z", "ylo", "x")
    return jax.shard_map(
        on_device,
        mesh=fine,
        in_specs=(
            P("img", None),
            P(),
            P("img", None, aux, "kp"),
            P(("kp", "img"), None, None, aux),
        ),
        out_specs=(P(("kp", "img"), None, None, aux, None), P()),
        check_vma=False,
    )
```

```python
import math

import jax
import jax.numpy as jnp
import numpy as np
from jax import lax
from jax.experimental import pallas as pl
from jax.experimental.pallas import tpu as pltpu
from jax.sharding import Mesh
from jax.sharding import PartitionSpec as P

NAO = 512
NAUX = 4096
NK = 8
MESH = 2
ROWS = 4
LANES = 128
JOIN_COST = 30_000_000_000

ANGLE = np.float32(math.pi / MESH)
COS = [float(np.cos(ANGLE * np.float32(t), dtype=np.float32)) for t in range(2 * MESH)]
SIN = [float(np.sin(ANGLE * np.float32(t), dtype=np.float32)) for t in range(2 * MESH)]
HBM = pl.BlockSpec(memory_space=pltpu.HBM)
VMEM = pl.BlockSpec(memory_space=pltpu.VMEM)


def pick(turns, values):
    out = jnp.full(turns.shape, values[0], jnp.float32)
    for t in range(1, 2 * MESH):
        out = jnp.where(turns == t, values[t], out)
    return out.astype(jnp.bfloat16).astype(jnp.float32)


STEP = 32


def phase_sums(blocks, table, j, c):
    acc = None
    for r, block in enumerate(blocks):
        term = table[j, c, r : r + 1, :] * block
        acc = term if acc is None else acc + term
    return acc.astype(jnp.bfloat16)


def pack_kernel(
    kpts_hbm, lat_hbm, x_hbm, dens_hbm, packed_hbm, spread_hbm, own_table,
    kpts_ref, lat_ref, dens_ref, phases_ref, small_sems, x_sems, out_sem, spread_sems,
):
    img, kp = lax.axis_index("img"), lax.axis_index("kp")
    images, rows, _ = x_hbm.shape
    kp_count = own_table.shape[0]
    small = [
        pltpu.make_async_copy(src, dst, small_sems.at[i])
        for i, (src, dst) in enumerate(
            ((kpts_hbm, kpts_ref), (lat_hbm, lat_ref), (dens_hbm, dens_ref))
        )
    ]
    whole = [
        pltpu.make_async_copy(x_hbm.at[r], packed_hbm.at[pl.ds(r * rows, rows)], x_sems.at[r])
        for r in range(images)
    ]
    fan = [
        pltpu.make_async_copy(dens_ref, spread_hbm.at[i], spread_sems.at[i])
        for i in range(spread_hbm.shape[0])
    ]
    below = pltpu.make_async_copy(
        phases_ref, packed_hbm.at[pl.ds(images * rows, phases_ref.shape[0])], out_sem
    )
    for copy in small + whole:
        copy.start()
    small[0].wait()
    small[1].wait()
    sub = lax.broadcasted_iota(jnp.int32, (images, LANES), 0)
    lat = []
    for a in range(3):
        column = jnp.zeros((images, LANES), jnp.int32)
        for r in range(images):
            column = jnp.where(sub == r, lat_ref[a, r], column)
        lat.append(column)
    for j in range(kp_count):
        for mine in (False, True):
            k = 2 * jnp.bitwise_xor(kp, j) + (img if mine else 1 - img)
            turns = jnp.zeros((images, LANES), jnp.int32)
            for a in range(3):
                turns = turns + (2 * kpts_ref[a, k] + 1) * lat[a]
            turns = jnp.bitwise_and(turns, 2 * MESH - 1)
            both = [pick(turns, COS), pick(turns, SIN)]
            if mine:
                own_table[j, 0], own_table[j, 1] = both
            else:
                at = pl.ds(2 * j * images, 2 * images)
                phases_ref[at, :] = jnp.concatenate(both, axis=0).astype(jnp.bfloat16)
    below.start()
    small[2].wait()
    for copy in fan:
        copy.start()
    for copy in whole + fan + [below]:
        copy.wait()


def pack(kpoints, lattice, x, piece, kp_count, near):
    images, rows, cols = x.shape
    phase_rows = 2 * kp_count * images
    table = jax.ShapeDtypeStruct((kp_count, 2, images, LANES), jnp.float32)
    return pl.pallas_call(
        pack_kernel,
        out_shape=(
            jax.ShapeDtypeStruct((images * rows + phase_rows, cols), x.dtype),
            jax.ShapeDtypeStruct((near,) + piece.shape, piece.dtype),
            table,
        ),
        in_specs=[HBM] * 4,
        out_specs=(HBM, HBM, VMEM),
        scratch_shapes=[
            pltpu.SMEM(kpoints.shape[::-1], jnp.int32),
            pltpu.SMEM(lattice.shape[::-1], jnp.int32),
            pltpu.VMEM(piece.shape, piece.dtype),
            pltpu.VMEM((phase_rows, cols), x.dtype),
            pltpu.SemaphoreType.DMA((3,)),
            pltpu.SemaphoreType.DMA((images,)),
            pltpu.SemaphoreType.DMA,
            pltpu.SemaphoreType.DMA((near,)),
        ],
        compiler_params=pltpu.CompilerParams(vmem_limit_bytes=56 * 1024 * 1024),
        name="pack",
    )(kpoints.T, lattice.T, x, piece)


def fit_kernel(own_table, x_ref, got_ref, *refs):
    *outs, got_table = refs
    images, rows, _ = x_ref.shape
    for j in range(len(outs)):
        at = pl.ds(images * rows + 2 * j * images, 2 * images)
        both = got_ref[at, :].astype(jnp.float32)
        got_table[j, 0], got_table[j, 1] = both[:images], both[images:]

    def body(t, carry):
        at = pl.ds(pl.multiple_of(t * STEP, STEP), STEP)
        sums = []
        for group, table in enumerate((own_table, got_table)):
            blocks = []
            for r in range(images):
                if group == 0:
                    block = x_ref[r, at, :]
                else:
                    block = got_ref[pl.ds(pl.multiple_of(r * rows + t * STEP, STEP), STEP), :]
                blocks.append(block.astype(jnp.float32))
            sums.append(
                [phase_sums(blocks, table, j, c) for j in range(len(outs)) for c in range(2)]
            )
        for m, (p, q) in enumerate(zip(*sums)):
            total = p.astype(jnp.float32) + q.astype(jnp.float32)
            outs[m // 2][m % 2, at, :] = total.astype(jnp.bfloat16)
        return carry

    lax.fori_loop(0, rows // STEP, body, 0)


def fit(table, x, got):
    _, rows, cols = x.shape
    out = jax.ShapeDtypeStruct((2, rows, cols), x.dtype)
    return pl.pallas_call(
        fit_kernel,
        out_shape=[out] * table.shape[0],
        in_specs=[VMEM] * 3,
        out_specs=[VMEM] * table.shape[0],
        scratch_shapes=[pltpu.VMEM(table.shape, table.dtype)],
        compiler_params=pltpu.CompilerParams(vmem_limit_bytes=16 * 1024 * 1024),
        name="fit",
    )(table, x, got)


def spread_kernel(x_ref, o_hbm, sems):
    me = lax.axis_index("x")
    count = o_hbm.shape[0]
    copies = [
        pltpu.make_async_copy(x_ref, o_hbm.at[jnp.bitwise_xor(me, i)], sems.at[i])
        for i in range(1, count)
    ]
    for copy in copies:
        copy.start()
    for copy in copies:
        copy.wait()


def spread(x, count):
    return pl.pallas_call(
        spread_kernel,
        out_shape=jax.ShapeDtypeStruct((count,) + x.shape, x.dtype),
        in_specs=[VMEM],
        out_specs=HBM,
        scratch_shapes=[pltpu.SemaphoreType.DMA((count,))],
        compiler_params=pltpu.CompilerParams(vmem_limit_bytes=16 * 1024 * 1024),
        name="spread",
    )(x)


def nt(a, b):
    return lax.dot_general(a, b, (((1,), (1,)), ((), ())), preferred_element_type=jnp.float32)


def join_kernel(*refs):
    out_ref = refs[-1]
    for j, ref in enumerate(refs[:-1]):
        out_ref[j] = ref[...]


def join(blocks):
    out = jax.ShapeDtypeStruct((len(blocks),) + blocks[0].shape, jnp.bfloat16)
    return pl.pallas_call(
        join_kernel,
        out_shape=out,
        in_specs=[VMEM] * len(blocks),
        out_specs=VMEM,
        compiler_params=pltpu.CompilerParams(vmem_limit_bytes=16 * 1024 * 1024),
        cost_estimate=pl.CostEstimate(
            flops=JOIN_COST, bytes_accessed=2 * out.size * 2, transcendentals=0
        ),
        name="join",
    )(*blocks)


def rows_kernel(
    first_ref, last_ref, own_ref, g_ref, w_hbm, part_ref, dens, fit, w_ref, sems
):
    xs, groups, pack, _ = g_ref.shape
    half = pack // 2
    kp = lax.axis_index("kp")
    width = last_ref.shape[2]
    early = first_ref.shape[0]
    for j in range(early + 1):
        ref = first_ref.at[j] if j < early else last_ref
        at = pl.ds(pl.multiple_of(jnp.bitwise_xor(kp, j) * width, width), width)
        for c in range(2):
            fit[c, :, at] = ref[c]
    me = lax.axis_index("x")
    for g in range(groups):
        mine = own_ref[g]
        for x in range(0, xs, 2):
            first = jnp.where(me == x, mine, g_ref[x, g])
            second = jnp.where(me == x + 1, mine, g_ref[x + 1, g])
            at = pl.ds((g * xs + x) * half, pack)
            for c in range(2):
                cut = slice(c * half, (c + 1) * half)
                dens[c, at, :] = jnp.concatenate([first[cut], second[cut]], axis=0)
    f_real, f_imag = fit[0], fit[1]
    d_real, d_imag = dens[0], dens[1]
    out = [pltpu.make_async_copy(w_ref.at[c], w_hbm.at[c], sems.at[c]) for c in range(2)]
    w_real = (nt(f_real, d_real) - nt(f_imag, d_imag)).astype(jnp.bfloat16)
    w_ref[0] = w_real
    out[0].start()
    w_imag = (nt(f_real, d_imag) + nt(f_imag, d_real)).astype(jnp.bfloat16)
    w_ref[1] = w_imag
    out[1].start()
    n = f_real.shape[0]
    aux = n // ROWS
    row = lax.broadcasted_iota(jnp.int32, (n, n), 0)
    col = lax.broadcasted_iota(jnp.int32, (n, n), 1)
    same = jnp.bitwise_and(row, aux - 1) == jnp.bitwise_and(col, aux - 1)
    sums = []
    for gram in (
        nt(w_real, f_real) + nt(w_imag, f_imag),
        nt(w_imag, f_real) - nt(w_real, f_imag),
    ):
        kept = jnp.where(same, gram, 0.0)
        for i in range(ROWS):
            sums.append(jnp.sum(kept[i * aux : (i + 1) * aux], axis=0, keepdims=True))
    stacked = jnp.concatenate(sums, axis=0)
    count = 2 * ROWS
    lane = lax.broadcasted_iota(jnp.int32, (count, LANES), 1)
    sub = lax.broadcasted_iota(jnp.int32, (count, LANES), 0)
    terms = jnp.zeros((count, LANES), jnp.float32)
    at_col = lax.broadcasted_iota(jnp.int32, (count, n), 1)
    for j in range(ROWS):
        mine = jnp.logical_and(at_col >= j * aux, at_col < (j + 1) * aux)
        total = jnp.sum(jnp.where(mine, stacked, 0.0), axis=1, keepdims=True)
        terms = terms + jnp.where(lane == sub * ROWS + j, total, 0.0)
    part_ref[...] = jnp.sum(terms, axis=0, keepdims=True)
    out[0].wait()
    out[1].wait()


def exchange(first, last, own, g):
    _, rows, width = last.shape
    n = width * (first.shape[0] + 1)
    wide = jax.ShapeDtypeStruct((2, rows, n), jnp.bfloat16)
    return pl.pallas_call(
        rows_kernel,
        out_shape=(wide, jax.ShapeDtypeStruct((1, LANES), jnp.float32)),
        in_specs=[VMEM] * 4,
        out_specs=(HBM, VMEM),
        scratch_shapes=[
            pltpu.VMEM((2, n, n), jnp.bfloat16),
            pltpu.VMEM(wide.shape, wide.dtype),
            pltpu.VMEM(wide.shape, wide.dtype),
            pltpu.SemaphoreType.DMA((2,)),
        ],
        compiler_params=pltpu.CompilerParams(vmem_limit_bytes=32 * 1024 * 1024),
        name="exchange",
    )(first, last, own, g)


def terms_over(part, axes):
    count = lax.axis_size(axes)
    block = jnp.broadcast_to(part[None], (count,) + part.shape)
    return lax.all_to_all(block, axes, 0, 0, tiled=True)


def on_device(lattice, kpoints, tensors, density):
    kp_count = lax.axis_size("kp")
    images, rows, aux_local, orb_local = tensors.shape
    n = orb_local * kp_count
    near, xs = lax.axis_size(("z", "ylo")), lax.axis_size("x")
    piece = density[0].transpose(0, 2, 1).reshape(-1, n)
    images_held = tensors.reshape(images, -1, orb_local)
    packed, block, table = pack(kpoints, lattice, images_held, piece, kp_count, near)
    got = lax.ppermute(packed, "img", [(0, 1), (1, 0)])
    own = lax.all_to_all(block, ("z", "ylo"), 0, 0, tiled=True)
    fitted = fit(table, images_held, got)
    fitted = [
        block if j == 0 else lax.ppermute(block, "kp", [(i, i ^ j) for i in range(kp_count)])
        for j, block in enumerate(fitted)
    ]
    dens = lax.all_to_all(spread(own, xs), "x", 0, 0, tiled=True)

    products, part = exchange(join(fitted[:-1]), fitted[-1], own, dens)
    part = jnp.sum(terms_over(part, ("z", "img")), axis=0)
    part = jnp.sum(terms_over(part, ("x", "ylo", "kp")), axis=0)
    scale = 1.0 / math.sqrt(NK * NAUX * NAO)
    tile = part[0, : 2 * ROWS * ROWS].reshape(2, ROWS, ROWS) * scale
    return products.reshape(1, 2, rows, aux_local, n), tile


def solution(mesh):
    fine = Mesh(mesh.devices.reshape(8, 2, 4, 4, 2), ("z", "ylo", "x", "kp", "img"))
    aux = ("z", "ylo", "x")
    return jax.shard_map(
        on_device,
        mesh=fine,
        in_specs=(
            P("img", None),
            P(),
            P("img", None, aux, "kp"),
            P(("kp", "img"), None, None, aux),
        ),
        out_specs=(P(("kp", "img"), None, None, aux, None), P()),
        check_vma=False,
    )
```

```python
import math

import jax
import jax.numpy as jnp
import numpy as np
from jax import lax
from jax.experimental import pallas as pl
from jax.experimental.pallas import tpu as pltpu
from jax.sharding import Mesh
from jax.sharding import PartitionSpec as P

NAO = 512
NAUX = 4096
NK = 8
MESH = 2
ROWS = 4
LANES = 128
EARLY, LATE = (0, 1, 3), (2,)
JOIN_COST = 30_000_000_000

ANGLE = np.float32(math.pi / MESH)
COS = [float(np.cos(ANGLE * np.float32(t), dtype=np.float32)) for t in range(2 * MESH)]
SIN = [float(np.sin(ANGLE * np.float32(t), dtype=np.float32)) for t in range(2 * MESH)]
HBM = pl.BlockSpec(memory_space=pltpu.HBM)
VMEM = pl.BlockSpec(memory_space=pltpu.VMEM)


def pick(turns, values):
    out = jnp.full(turns.shape, values[0], jnp.float32)
    for t in range(1, 2 * MESH):
        out = jnp.where(turns == t, values[t], out)
    return out.astype(jnp.bfloat16).astype(jnp.float32)


STEP = 32
CUTS = 2


def phase_sums(blocks, table, j, c):
    acc = None
    for r, block in enumerate(blocks):
        term = table[j, c, r : r + 1, :] * block
        acc = term if acc is None else acc + term
    return acc.astype(jnp.bfloat16)


def pack_kernel(
    kpts_hbm, lat_hbm, x_hbm, dens_hbm, packed_hbm, spread_hbm, own_table,
    kpts_ref, lat_ref, dens_ref, fan_ref, packed_ref, small_sems, x_sems, out_sems, spread_sem,
):
    img, kp = lax.axis_index("img"), lax.axis_index("kp")
    kp_count, _, images, _ = own_table.shape
    above = x_hbm.shape[0]
    size = above // CUTS
    small = [
        pltpu.make_async_copy(src, dst, small_sems.at[i])
        for i, (src, dst) in enumerate(
            ((kpts_hbm, kpts_ref), (lat_hbm, lat_ref), (dens_hbm, dens_ref))
        )
    ]
    parts = [pl.ds(r * size, size) for r in range(CUTS)]
    parts.append(pl.ds(above, 2 * kp_count * images))
    whole = [
        pltpu.make_async_copy(x_hbm.at[at], packed_ref.at[at], x_sems.at[r])
        for r, at in enumerate(parts[:CUTS])
    ]
    out = [
        pltpu.make_async_copy(packed_ref.at[at], packed_hbm.at[at], out_sems.at[r])
        for r, at in enumerate(parts)
    ]
    fan = pltpu.make_async_copy(fan_ref, spread_hbm, spread_sem)
    for copy in small + whole:
        copy.start()
    small[0].wait()
    small[1].wait()
    sub = lax.broadcasted_iota(jnp.int32, (images, LANES), 0)
    lat = []
    for a in range(3):
        column = jnp.zeros((images, LANES), jnp.int32)
        for r in range(images):
            column = jnp.where(sub == r, lat_ref[a, r], column)
        lat.append(column)
    for j in range(kp_count):
        for mine in (False, True):
            k = 2 * jnp.bitwise_xor(kp, j) + (img if mine else 1 - img)
            turns = jnp.zeros((images, LANES), jnp.int32)
            for a in range(3):
                turns = turns + (2 * kpts_ref[a, k] + 1) * lat[a]
            turns = jnp.bitwise_and(turns, 2 * MESH - 1)
            both = [pick(turns, COS), pick(turns, SIN)]
            if mine:
                own_table[j, 0], own_table[j, 1] = both
            else:
                at = pl.ds(above + 2 * j * images, 2 * images)
                packed_ref[at, :] = jnp.concatenate(both, axis=0).astype(jnp.bfloat16)
    out[CUTS].start()
    small[2].wait()
    for i in range(fan_ref.shape[0]):
        fan_ref[i] = dens_ref[...]
    fan.start()
    for r in range(CUTS):
        whole[r].wait()
        out[r].start()
    for copy in out + [fan]:
        copy.wait()


def pack(kpoints, lattice, x, piece, kp_count, near):
    images, rows, cols = x.shape
    phase_rows = 2 * kp_count * images
    table = jax.ShapeDtypeStruct((kp_count, 2, images, LANES), jnp.float32)
    return pl.pallas_call(
        pack_kernel,
        out_shape=(
            jax.ShapeDtypeStruct((images * rows + phase_rows, cols), x.dtype),
            jax.ShapeDtypeStruct((near,) + piece.shape, piece.dtype),
            table,
        ),
        in_specs=[HBM] * 4,
        out_specs=(HBM, HBM, VMEM),
        scratch_shapes=[
            pltpu.SMEM(kpoints.shape[::-1], jnp.int32),
            pltpu.SMEM(lattice.shape[::-1], jnp.int32),
            pltpu.VMEM(piece.shape, piece.dtype),
            pltpu.VMEM((near,) + piece.shape, piece.dtype),
            pltpu.VMEM((images * rows + phase_rows, cols), x.dtype),
            pltpu.SemaphoreType.DMA((3,)),
            pltpu.SemaphoreType.DMA((CUTS,)),
            pltpu.SemaphoreType.DMA((CUTS + 1,)),
            pltpu.SemaphoreType.DMA,
        ],
        compiler_params=pltpu.CompilerParams(vmem_limit_bytes=56 * 1024 * 1024),
        name="pack",
    )(kpoints.T, lattice.T, x.reshape(-1, cols), piece)


def fit_kernel(own_table, x_ref, got_ref, *refs):
    *outs, got_table = refs
    images, rows, _ = x_ref.shape
    for j in range(len(outs)):
        at = pl.ds(images * rows + 2 * j * images, 2 * images)
        both = got_ref[at, :].astype(jnp.float32)
        got_table[j, 0], got_table[j, 1] = both[:images], both[images:]

    def body(t, carry):
        at = pl.ds(pl.multiple_of(t * STEP, STEP), STEP)
        sums = []
        for group, table in enumerate((own_table, got_table)):
            blocks = []
            for r in range(images):
                if group == 0:
                    block = x_ref[r, at, :]
                else:
                    block = got_ref[pl.ds(pl.multiple_of(r * rows + t * STEP, STEP), STEP), :]
                blocks.append(block.astype(jnp.float32))
            sums.append(
                [phase_sums(blocks, table, j, c) for j in range(len(outs)) for c in range(2)]
            )
        for m, (p, q) in enumerate(zip(*sums)):
            total = p.astype(jnp.float32) + q.astype(jnp.float32)
            outs[m // 2][m % 2, at, :] = total.astype(jnp.bfloat16)
        return carry

    lax.fori_loop(0, rows // STEP, body, 0)


def fit(table, x, got):
    _, rows, cols = x.shape
    out = jax.ShapeDtypeStruct((2, rows, cols), x.dtype)
    return pl.pallas_call(
        fit_kernel,
        out_shape=[out] * table.shape[0],
        in_specs=[VMEM] * 3,
        out_specs=[VMEM] * table.shape[0],
        scratch_shapes=[pltpu.VMEM(table.shape, table.dtype)],
        compiler_params=pltpu.CompilerParams(vmem_limit_bytes=16 * 1024 * 1024),
        name="fit",
    )(table, x, got)


def spread_kernel(x_ref, o_hbm, sems):
    me = lax.axis_index("x")
    count = o_hbm.shape[0]
    copies = [
        pltpu.make_async_copy(x_ref, o_hbm.at[jnp.bitwise_xor(me, i)], sems.at[i])
        for i in range(1, count)
    ]
    for copy in copies:
        copy.start()
    for copy in copies:
        copy.wait()


def spread(x, count):
    return pl.pallas_call(
        spread_kernel,
        out_shape=jax.ShapeDtypeStruct((count,) + x.shape, x.dtype),
        in_specs=[VMEM],
        out_specs=HBM,
        scratch_shapes=[pltpu.SemaphoreType.DMA((count,))],
        compiler_params=pltpu.CompilerParams(vmem_limit_bytes=16 * 1024 * 1024),
        name="spread",
    )(x)


def nt(a, b):
    return lax.dot_general(a, b, (((1,), (1,)), ((), ())), preferred_element_type=jnp.float32)


def join_kernel(*refs):
    out_ref = refs[-1]
    for j, ref in enumerate(refs[:-1]):
        out_ref[j] = ref[...]


def join(blocks):
    out = jax.ShapeDtypeStruct((len(blocks),) + blocks[0].shape, jnp.bfloat16)
    return pl.pallas_call(
        join_kernel,
        out_shape=out,
        in_specs=[VMEM] * len(blocks),
        out_specs=VMEM,
        compiler_params=pltpu.CompilerParams(vmem_limit_bytes=16 * 1024 * 1024),
        cost_estimate=pl.CostEstimate(
            flops=JOIN_COST, bytes_accessed=2 * out.size * 2, transcendentals=0
        ),
        name="join",
    )(*blocks)


def rows_kernel(first_ref, *refs):
    late, refs = refs[: len(LATE)], refs[len(LATE) :]
    own_ref, g_ref, w_hbm, part_ref, dens, fit, w_ref, sems = refs
    xs, groups, pack, _ = g_ref.shape
    half = pack // 2
    kp = lax.axis_index("kp")
    width = first_ref.shape[3]
    blocks = [(j, first_ref.at[i]) for i, j in enumerate(EARLY)] + list(zip(LATE, late))
    for j, ref in blocks:
        at = pl.ds(pl.multiple_of(jnp.bitwise_xor(kp, j) * width, width), width)
        for c in range(2):
            fit[c, :, at] = ref[c]
    me = lax.axis_index("x")
    for g in range(groups):
        mine = own_ref[g]
        for x in range(0, xs, 2):
            first = jnp.where(me == x, mine, g_ref[x, g])
            second = jnp.where(me == x + 1, mine, g_ref[x + 1, g])
            at = pl.ds((g * xs + x) * half, pack)
            for c in range(2):
                cut = slice(c * half, (c + 1) * half)
                dens[c, at, :] = jnp.concatenate([first[cut], second[cut]], axis=0)
    f_real, f_imag = fit[0], fit[1]
    d_real, d_imag = dens[0], dens[1]
    out = [pltpu.make_async_copy(w_ref.at[c], w_hbm.at[c], sems.at[c]) for c in range(2)]
    w_real = (nt(f_real, d_real) - nt(f_imag, d_imag)).astype(jnp.bfloat16)
    w_ref[0] = w_real
    out[0].start()
    w_imag = (nt(f_real, d_imag) + nt(f_imag, d_real)).astype(jnp.bfloat16)
    w_ref[1] = w_imag
    out[1].start()
    n = f_real.shape[0]
    aux = n // ROWS
    row = lax.broadcasted_iota(jnp.int32, (n, n), 0)
    col = lax.broadcasted_iota(jnp.int32, (n, n), 1)
    same = jnp.bitwise_and(row, aux - 1) == jnp.bitwise_and(col, aux - 1)
    sums = []
    for gram in (
        nt(w_real, f_real) + nt(w_imag, f_imag),
        nt(w_imag, f_real) - nt(w_real, f_imag),
    ):
        kept = jnp.where(same, gram, 0.0)
        for i in range(ROWS):
            sums.append(jnp.sum(kept[i * aux : (i + 1) * aux], axis=0, keepdims=True))
    stacked = jnp.concatenate(sums, axis=0)
    count = 2 * ROWS
    lane = lax.broadcasted_iota(jnp.int32, (count, LANES), 1)
    sub = lax.broadcasted_iota(jnp.int32, (count, LANES), 0)
    terms = jnp.zeros((count, LANES), jnp.float32)
    at_col = lax.broadcasted_iota(jnp.int32, (count, n), 1)
    for j in range(ROWS):
        mine = jnp.logical_and(at_col >= j * aux, at_col < (j + 1) * aux)
        total = jnp.sum(jnp.where(mine, stacked, 0.0), axis=1, keepdims=True)
        terms = terms + jnp.where(lane == sub * ROWS + j, total, 0.0)
    part_ref[...] = jnp.sum(terms, axis=0, keepdims=True)
    out[0].wait()
    out[1].wait()


def exchange(first, late, own, g):
    _, _, rows, width = first.shape
    n = width * (len(EARLY) + len(LATE))
    wide = jax.ShapeDtypeStruct((2, rows, n), jnp.bfloat16)
    return pl.pallas_call(
        rows_kernel,
        out_shape=(wide, jax.ShapeDtypeStruct((1, LANES), jnp.float32)),
        in_specs=[VMEM] * (3 + len(LATE)),
        out_specs=(HBM, VMEM),
        scratch_shapes=[
            pltpu.VMEM((2, n, n), jnp.bfloat16),
            pltpu.VMEM(wide.shape, wide.dtype),
            pltpu.VMEM(wide.shape, wide.dtype),
            pltpu.SemaphoreType.DMA((2,)),
        ],
        compiler_params=pltpu.CompilerParams(vmem_limit_bytes=32 * 1024 * 1024),
        name="exchange",
    )(first, *late, own, g)


def terms_over(part, axes):
    count = lax.axis_size(axes)
    block = jnp.broadcast_to(part[None], (count,) + part.shape)
    return lax.all_to_all(block, axes, 0, 0, tiled=True)


def on_device(lattice, kpoints, tensors, density):
    kp_count = lax.axis_size("kp")
    images, rows, aux_local, orb_local = tensors.shape
    n = orb_local * kp_count
    near, xs = lax.axis_size(("z", "ylo")), lax.axis_size("x")
    piece = density[0].transpose(0, 2, 1).reshape(-1, n)
    images_held = tensors.reshape(images, -1, orb_local)
    packed, block, table = pack(kpoints, lattice, images_held, piece, kp_count, near)
    got = lax.ppermute(packed, "img", [(0, 1), (1, 0)])
    own = lax.all_to_all(block, ("z", "ylo"), 0, 0, tiled=True)
    fitted = fit(table, images_held, got)
    fitted = [
        block if j == 0 else lax.ppermute(block, "kp", [(i, i ^ j) for i in range(kp_count)])
        for j, block in enumerate(fitted)
    ]
    dens = lax.all_to_all(spread(own, xs), "x", 0, 0, tiled=True)

    products, part = exchange(join([fitted[j] for j in EARLY]), [fitted[j] for j in LATE], own, dens)
    part = jnp.sum(terms_over(part, ("z", "img")), axis=0)
    part = jnp.sum(terms_over(part, ("x", "ylo", "kp")), axis=0)
    scale = 1.0 / math.sqrt(NK * NAUX * NAO)
    tile = part[0, : 2 * ROWS * ROWS].reshape(2, ROWS, ROWS) * scale
    return products.reshape(1, 2, rows, aux_local, n), tile


def solution(mesh):
    fine = Mesh(mesh.devices.reshape(8, 2, 4, 4, 2), ("z", "ylo", "x", "kp", "img"))
    aux = ("z", "ylo", "x")
    return jax.shard_map(
        on_device,
        mesh=fine,
        in_specs=(
            P("img", None),
            P(),
            P("img", None, aux, "kp"),
            P(("kp", "img"), None, None, aux),
        ),
        out_specs=(P(("kp", "img"), None, None, aux, None), P()),
        check_vma=False,
    )
```

```python
import math

import jax
import jax.numpy as jnp
import numpy as np
from jax import lax
from jax.experimental import pallas as pl
from jax.experimental.pallas import tpu as pltpu
from jax.sharding import Mesh
from jax.sharding import PartitionSpec as P

NAO = 512
NAUX = 4096
NK = 8
MESH = 2
ROWS = 4
LANES = 128
EARLY, LATE = (0, 1, 3), (2,)
JOIN_COST = 30_000_000_000

ANGLE = np.float32(math.pi / MESH)
COS = [float(np.cos(ANGLE * np.float32(t), dtype=np.float32)) for t in range(2 * MESH)]
SIN = [float(np.sin(ANGLE * np.float32(t), dtype=np.float32)) for t in range(2 * MESH)]
HBM = pl.BlockSpec(memory_space=pltpu.HBM)
VMEM = pl.BlockSpec(memory_space=pltpu.VMEM)


def pick(turns, values):
    out = jnp.full(turns.shape, values[0], jnp.float32)
    for t in range(1, 2 * MESH):
        out = jnp.where(turns == t, values[t], out)
    return out.astype(jnp.bfloat16).astype(jnp.float32)


STEP = 32
CUTS = 2


def phase_sums(blocks, table, j, c):
    acc = None
    for r, block in enumerate(blocks):
        term = table[j, c, r : r + 1, :] * block
        acc = term if acc is None else acc + term
    return acc.astype(jnp.bfloat16)


def pack_kernel(
    kpts_hbm, lat_hbm, x_hbm, dens_hbm, packed_hbm, spread_hbm, own_table,
    kpts_ref, lat_ref, dens_ref, fan_ref, packed_ref, small_sems, x_sems, out_sems, spread_sem,
):
    img, kp = lax.axis_index("img"), lax.axis_index("kp")
    kp_count, _, images, _ = own_table.shape
    above = x_hbm.shape[0]
    size = above // CUTS
    small = [
        pltpu.make_async_copy(src, dst, small_sems.at[i])
        for i, (src, dst) in enumerate(
            ((kpts_hbm, kpts_ref), (lat_hbm, lat_ref), (dens_hbm, dens_ref))
        )
    ]
    parts = [pl.ds(r * size, size) for r in range(CUTS)]
    parts.append(pl.ds(above, 2 * kp_count * images))
    whole = [
        pltpu.make_async_copy(x_hbm.at[at], packed_ref.at[at], x_sems.at[r])
        for r, at in enumerate(parts[:CUTS])
    ]
    out = [
        pltpu.make_async_copy(packed_ref.at[at], packed_hbm.at[at], out_sems.at[r])
        for r, at in enumerate(parts)
    ]
    fan = pltpu.make_async_copy(fan_ref, spread_hbm, spread_sem)
    for copy in small + whole:
        copy.start()
    small[0].wait()
    small[1].wait()
    sub = lax.broadcasted_iota(jnp.int32, (images, LANES), 0)
    lat = []
    for a in range(3):
        column = jnp.zeros((images, LANES), jnp.int32)
        for r in range(images):
            column = jnp.where(sub == r, lat_ref[a, r], column)
        lat.append(column)
    for j in range(kp_count):
        for mine in (False, True):
            k = 2 * jnp.bitwise_xor(kp, j) + (img if mine else 1 - img)
            turns = jnp.zeros((images, LANES), jnp.int32)
            for a in range(3):
                turns = turns + (2 * kpts_ref[a, k] + 1) * lat[a]
            turns = jnp.bitwise_and(turns, 2 * MESH - 1)
            both = [pick(turns, COS), pick(turns, SIN)]
            if mine:
                own_table[j, 0], own_table[j, 1] = both
            else:
                at = pl.ds(above + 2 * j * images, 2 * images)
                packed_ref[at, :] = jnp.concatenate(both, axis=0).astype(jnp.bfloat16)
    out[CUTS].start()
    small[2].wait()
    for i in range(fan_ref.shape[0]):
        fan_ref[i] = dens_ref[...]
    fan.start()
    for r in range(CUTS):
        whole[r].wait()
        out[r].start()
    for copy in out + [fan]:
        copy.wait()


def pack(kpoints, lattice, x, piece, kp_count, near):
    images, rows, cols = x.shape
    phase_rows = 2 * kp_count * images
    table = jax.ShapeDtypeStruct((kp_count, 2, images, LANES), jnp.float32)
    return pl.pallas_call(
        pack_kernel,
        out_shape=(
            jax.ShapeDtypeStruct((images * rows + phase_rows, cols), x.dtype),
            jax.ShapeDtypeStruct((near,) + piece.shape, piece.dtype),
            table,
        ),
        in_specs=[HBM] * 4,
        out_specs=(HBM, HBM, VMEM),
        scratch_shapes=[
            pltpu.SMEM(kpoints.shape[::-1], jnp.int32),
            pltpu.SMEM(lattice.shape[::-1], jnp.int32),
            pltpu.VMEM(piece.shape, piece.dtype),
            pltpu.VMEM((near,) + piece.shape, piece.dtype),
            pltpu.VMEM((images * rows + phase_rows, cols), x.dtype),
            pltpu.SemaphoreType.DMA((3,)),
            pltpu.SemaphoreType.DMA((CUTS,)),
            pltpu.SemaphoreType.DMA((CUTS + 1,)),
            pltpu.SemaphoreType.DMA,
        ],
        compiler_params=pltpu.CompilerParams(vmem_limit_bytes=56 * 1024 * 1024),
        name="pack",
    )(kpoints.T, lattice.T, x.reshape(-1, cols), piece)


def fit_kernel(own_table, x_ref, got_ref, *refs):
    *outs, got_table = refs
    images, rows, _ = x_ref.shape
    for j in range(len(outs)):
        at = pl.ds(images * rows + 2 * j * images, 2 * images)
        both = got_ref[at, :].astype(jnp.float32)
        got_table[j, 0], got_table[j, 1] = both[:images], both[images:]

    def body(t, carry):
        at = pl.ds(pl.multiple_of(t * STEP, STEP), STEP)
        sums = []
        for group, table in enumerate((own_table, got_table)):
            blocks = []
            for r in range(images):
                if group == 0:
                    block = x_ref[r, at, :]
                else:
                    block = got_ref[pl.ds(pl.multiple_of(r * rows + t * STEP, STEP), STEP), :]
                blocks.append(block.astype(jnp.float32))
            sums.append(
                [phase_sums(blocks, table, j, c) for j in range(len(outs)) for c in range(2)]
            )
        for m, (p, q) in enumerate(zip(*sums)):
            total = p.astype(jnp.float32) + q.astype(jnp.float32)
            outs[m // 2][m % 2, at, :] = total.astype(jnp.bfloat16)
        return carry

    lax.fori_loop(0, rows // STEP, body, 0)


def fit(table, x, got):
    _, rows, cols = x.shape
    out = jax.ShapeDtypeStruct((2, rows, cols), x.dtype)
    return pl.pallas_call(
        fit_kernel,
        out_shape=[out] * table.shape[0],
        in_specs=[VMEM] * 3,
        out_specs=[VMEM] * table.shape[0],
        scratch_shapes=[pltpu.VMEM(table.shape, table.dtype)],
        compiler_params=pltpu.CompilerParams(vmem_limit_bytes=16 * 1024 * 1024),
        name="fit",
    )(table, x, got)


def spread_kernel(x_ref, o_hbm, sems):
    me = lax.axis_index("x")
    count = o_hbm.shape[0]
    copies = [
        pltpu.make_async_copy(x_ref, o_hbm.at[jnp.bitwise_xor(me, i)], sems.at[i])
        for i in range(1, count)
    ]
    for copy in copies:
        copy.start()
    for copy in copies:
        copy.wait()


def spread(x, count):
    return pl.pallas_call(
        spread_kernel,
        out_shape=jax.ShapeDtypeStruct((count,) + x.shape, x.dtype),
        in_specs=[VMEM],
        out_specs=HBM,
        scratch_shapes=[pltpu.SemaphoreType.DMA((count,))],
        compiler_params=pltpu.CompilerParams(vmem_limit_bytes=16 * 1024 * 1024),
        name="spread",
    )(x)


def nt(a, b):
    return lax.dot_general(a, b, (((1,), (1,)), ((), ())), preferred_element_type=jnp.float32)


def join_kernel(*refs):
    out_ref = refs[-1]
    for j, ref in enumerate(refs[:-1]):
        out_ref[j] = ref[...]


def join(blocks):
    out = jax.ShapeDtypeStruct((len(blocks),) + blocks[0].shape, jnp.bfloat16)
    return pl.pallas_call(
        join_kernel,
        out_shape=out,
        in_specs=[VMEM] * len(blocks),
        out_specs=VMEM,
        compiler_params=pltpu.CompilerParams(vmem_limit_bytes=16 * 1024 * 1024),
        cost_estimate=pl.CostEstimate(
            flops=JOIN_COST, bytes_accessed=2 * out.size * 2, transcendentals=0
        ),
        name="join",
    )(*blocks)


def rows_kernel(first_ref, *refs):
    late, refs = refs[: len(LATE)], refs[len(LATE) :]
    own_ref, g_ref, w_ref, part_ref, dens, fit = refs
    xs, groups, pack, _ = g_ref.shape
    half = pack // 2
    kp = lax.axis_index("kp")
    width = first_ref.shape[3]
    blocks = [(j, first_ref.at[i]) for i, j in enumerate(EARLY)] + list(zip(LATE, late))
    for j, ref in blocks:
        at = pl.ds(pl.multiple_of(jnp.bitwise_xor(kp, j) * width, width), width)
        for c in range(2):
            fit[c, :, at] = ref[c]
    me = lax.axis_index("x")
    for g in range(groups):
        mine = own_ref[g]
        for x in range(0, xs, 2):
            first = jnp.where(me == x, mine, g_ref[x, g])
            second = jnp.where(me == x + 1, mine, g_ref[x + 1, g])
            at = pl.ds((g * xs + x) * half, pack)
            for c in range(2):
                cut = slice(c * half, (c + 1) * half)
                dens[c, at, :] = jnp.concatenate([first[cut], second[cut]], axis=0)
    f_real, f_imag = fit[0], fit[1]
    d_real, d_imag = dens[0], dens[1]
    w_real = (nt(f_real, d_real) - nt(f_imag, d_imag)).astype(jnp.bfloat16)
    w_ref[0] = w_real
    w_imag = (nt(f_real, d_imag) + nt(f_imag, d_real)).astype(jnp.bfloat16)
    w_ref[1] = w_imag
    n = f_real.shape[0]
    aux = n // ROWS
    row = lax.broadcasted_iota(jnp.int32, (n, n), 0)
    col = lax.broadcasted_iota(jnp.int32, (n, n), 1)
    same = jnp.bitwise_and(row, aux - 1) == jnp.bitwise_and(col, aux - 1)
    sums = []
    for gram in (
        nt(w_real, f_real) + nt(w_imag, f_imag),
        nt(w_imag, f_real) - nt(w_real, f_imag),
    ):
        kept = jnp.where(same, gram, 0.0)
        for i in range(ROWS):
            sums.append(jnp.sum(kept[i * aux : (i + 1) * aux], axis=0, keepdims=True))
    stacked = jnp.concatenate(sums, axis=0)
    count = 2 * ROWS
    lane = lax.broadcasted_iota(jnp.int32, (count, LANES), 1)
    sub = lax.broadcasted_iota(jnp.int32, (count, LANES), 0)
    terms = jnp.zeros((count, LANES), jnp.float32)
    at_col = lax.broadcasted_iota(jnp.int32, (count, n), 1)
    for j in range(ROWS):
        mine = jnp.logical_and(at_col >= j * aux, at_col < (j + 1) * aux)
        total = jnp.sum(jnp.where(mine, stacked, 0.0), axis=1, keepdims=True)
        terms = terms + jnp.where(lane == sub * ROWS + j, total, 0.0)
    part_ref[...] = jnp.sum(terms, axis=0, keepdims=True)


def exchange(first, late, own, g):
    _, _, rows, width = first.shape
    n = width * (len(EARLY) + len(LATE))
    wide = jax.ShapeDtypeStruct((2, rows, n), jnp.bfloat16)
    return pl.pallas_call(
        rows_kernel,
        out_shape=(wide, jax.ShapeDtypeStruct((1, LANES), jnp.float32)),
        in_specs=[VMEM] * (3 + len(LATE)),
        out_specs=(VMEM, VMEM),
        scratch_shapes=[
            pltpu.VMEM((2, n, n), jnp.bfloat16),
            pltpu.VMEM(wide.shape, wide.dtype),
        ],
        compiler_params=pltpu.CompilerParams(vmem_limit_bytes=32 * 1024 * 1024),
        name="exchange",
    )(first, *late, own, g)


def leave_kernel(w_ref, w_hbm, sems):
    copies = [pltpu.make_async_copy(w_ref.at[c], w_hbm.at[c], sems.at[c]) for c in range(2)]
    for copy in copies:
        copy.start()
    for copy in copies:
        copy.wait()


def leave(w):
    return pl.pallas_call(
        leave_kernel,
        out_shape=jax.ShapeDtypeStruct(w.shape, w.dtype),
        in_specs=[VMEM],
        out_specs=HBM,
        scratch_shapes=[pltpu.SemaphoreType.DMA((2,))],
        compiler_params=pltpu.CompilerParams(vmem_limit_bytes=16 * 1024 * 1024),
        cost_estimate=pl.CostEstimate(
            flops=JOIN_COST, bytes_accessed=4 * w.size, transcendentals=0
        ),
        name="leave",
    )(w)


def terms_over(part, axes):
    count = lax.axis_size(axes)
    block = jnp.broadcast_to(part[None], (count,) + part.shape)
    return lax.all_to_all(block, axes, 0, 0, tiled=True)


def on_device(lattice, kpoints, tensors, density):
    kp_count = lax.axis_size("kp")
    images, rows, aux_local, orb_local = tensors.shape
    n = orb_local * kp_count
    near, xs = lax.axis_size(("z", "ylo")), lax.axis_size("x")
    piece = density[0].transpose(0, 2, 1).reshape(-1, n)
    images_held = tensors.reshape(images, -1, orb_local)
    packed, block, table = pack(kpoints, lattice, images_held, piece, kp_count, near)
    got = lax.ppermute(packed, "img", [(0, 1), (1, 0)])
    own = lax.all_to_all(block, ("z", "ylo"), 0, 0, tiled=True)
    fitted = fit(table, images_held, got)
    fitted = [
        block if j == 0 else lax.ppermute(block, "kp", [(i, i ^ j) for i in range(kp_count)])
        for j, block in enumerate(fitted)
    ]
    dens = lax.all_to_all(spread(own, xs), "x", 0, 0, tiled=True)

    products, part = exchange(join([fitted[j] for j in EARLY]), [fitted[j] for j in LATE], own, dens)
    part = jnp.sum(terms_over(part, ("z", "img")), axis=0)
    part = jnp.sum(terms_over(part, ("x", "ylo", "kp")), axis=0)
    scale = 1.0 / math.sqrt(NK * NAUX * NAO)
    tile = part[0, : 2 * ROWS * ROWS].reshape(2, ROWS, ROWS) * scale
    return leave(products).reshape(1, 2, rows, aux_local, n), tile


def solution(mesh):
    fine = Mesh(mesh.devices.reshape(8, 2, 4, 4, 2), ("z", "ylo", "x", "kp", "img"))
    aux = ("z", "ylo", "x")
    return jax.shard_map(
        on_device,
        mesh=fine,
        in_specs=(
            P("img", None),
            P(),
            P("img", None, aux, "kp"),
            P(("kp", "img"), None, None, aux),
        ),
        out_specs=(P(("kp", "img"), None, None, aux, None), P()),
        check_vma=False,
    )
```

```python
import math

import jax
import jax.numpy as jnp
import numpy as np
from jax import lax
from jax.experimental import pallas as pl
from jax.experimental.pallas import tpu as pltpu
from jax.sharding import Mesh
from jax.sharding import PartitionSpec as P

NAO = 512
NAUX = 4096
NK = 8
MESH = 2
ROWS = 4
LANES = 128
EARLY, LATE = (0, 2), (1, 3)
JOIN_COST = 30_000_000_000

ANGLE = np.float32(math.pi / MESH)
COS = [float(np.cos(ANGLE * np.float32(t), dtype=np.float32)) for t in range(2 * MESH)]
SIN = [float(np.sin(ANGLE * np.float32(t), dtype=np.float32)) for t in range(2 * MESH)]
HBM = pl.BlockSpec(memory_space=pltpu.HBM)
VMEM = pl.BlockSpec(memory_space=pltpu.VMEM)


def pick(turns, values):
    out = jnp.full(turns.shape, values[0], jnp.float32)
    for t in range(1, 2 * MESH):
        out = jnp.where(turns == t, values[t], out)
    return out.astype(jnp.bfloat16).astype(jnp.float32)


STEP = 32
CUTS = 2


def phase_sums(blocks, table, j, c):
    acc = None
    for r, block in enumerate(blocks):
        term = table[j, c, r : r + 1, :] * block
        acc = term if acc is None else acc + term
    return acc.astype(jnp.bfloat16)


def pack_kernel(
    kpts_hbm, lat_hbm, x_hbm, dens_hbm, packed_hbm, spread_hbm, own_table,
    kpts_ref, lat_ref, dens_ref, fan_ref, packed_ref, small_sems, x_sems, out_sems, spread_sem,
):
    img, kp = lax.axis_index("img"), lax.axis_index("kp")
    kp_count, _, images, _ = own_table.shape
    above = x_hbm.shape[0]
    size = above // CUTS
    small = [
        pltpu.make_async_copy(src, dst, small_sems.at[i])
        for i, (src, dst) in enumerate(
            ((kpts_hbm, kpts_ref), (lat_hbm, lat_ref), (dens_hbm, dens_ref))
        )
    ]
    parts = [pl.ds(r * size, size) for r in range(CUTS)]
    parts.append(pl.ds(above, 2 * kp_count * images))
    whole = [
        pltpu.make_async_copy(x_hbm.at[at], packed_ref.at[at], x_sems.at[r])
        for r, at in enumerate(parts[:CUTS])
    ]
    out = [
        pltpu.make_async_copy(packed_ref.at[at], packed_hbm.at[at], out_sems.at[r])
        for r, at in enumerate(parts)
    ]
    fan = pltpu.make_async_copy(fan_ref, spread_hbm, spread_sem)
    for copy in small + whole:
        copy.start()
    small[0].wait()
    small[1].wait()
    sub = lax.broadcasted_iota(jnp.int32, (images, LANES), 0)
    lat = []
    for a in range(3):
        column = jnp.zeros((images, LANES), jnp.int32)
        for r in range(images):
            column = jnp.where(sub == r, lat_ref[a, r], column)
        lat.append(column)
    for j in range(kp_count):
        for mine in (False, True):
            k = 2 * jnp.bitwise_xor(kp, j) + (img if mine else 1 - img)
            turns = jnp.zeros((images, LANES), jnp.int32)
            for a in range(3):
                turns = turns + (2 * kpts_ref[a, k] + 1) * lat[a]
            turns = jnp.bitwise_and(turns, 2 * MESH - 1)
            both = [pick(turns, COS), pick(turns, SIN)]
            if mine:
                own_table[j, 0], own_table[j, 1] = both
            else:
                at = pl.ds(above + 2 * j * images, 2 * images)
                packed_ref[at, :] = jnp.concatenate(both, axis=0).astype(jnp.bfloat16)
    out[CUTS].start()
    small[2].wait()
    for i in range(fan_ref.shape[0]):
        fan_ref[i] = dens_ref[...]
    fan.start()
    for r in range(CUTS):
        whole[r].wait()
        out[r].start()
    for copy in out + [fan]:
        copy.wait()


def pack(kpoints, lattice, x, piece, kp_count, near):
    images, rows, cols = x.shape
    phase_rows = 2 * kp_count * images
    table = jax.ShapeDtypeStruct((kp_count, 2, images, LANES), jnp.float32)
    return pl.pallas_call(
        pack_kernel,
        out_shape=(
            jax.ShapeDtypeStruct((images * rows + phase_rows, cols), x.dtype),
            jax.ShapeDtypeStruct((near,) + piece.shape, piece.dtype),
            table,
        ),
        in_specs=[HBM] * 4,
        out_specs=(HBM, HBM, VMEM),
        scratch_shapes=[
            pltpu.SMEM(kpoints.shape[::-1], jnp.int32),
            pltpu.SMEM(lattice.shape[::-1], jnp.int32),
            pltpu.VMEM(piece.shape, piece.dtype),
            pltpu.VMEM((near,) + piece.shape, piece.dtype),
            pltpu.VMEM((images * rows + phase_rows, cols), x.dtype),
            pltpu.SemaphoreType.DMA((3,)),
            pltpu.SemaphoreType.DMA((CUTS,)),
            pltpu.SemaphoreType.DMA((CUTS + 1,)),
            pltpu.SemaphoreType.DMA,
        ],
        compiler_params=pltpu.CompilerParams(vmem_limit_bytes=56 * 1024 * 1024),
        name="pack",
    )(kpoints.T, lattice.T, x.reshape(-1, cols), piece)


def fit_kernel(own_table, x_ref, got_ref, *refs):
    *outs, got_table = refs
    images, rows, _ = x_ref.shape
    for j in range(len(outs)):
        at = pl.ds(images * rows + 2 * j * images, 2 * images)
        both = got_ref[at, :].astype(jnp.float32)
        got_table[j, 0], got_table[j, 1] = both[:images], both[images:]

    def body(t, carry):
        at = pl.ds(pl.multiple_of(t * STEP, STEP), STEP)
        sums = []
        for group, table in enumerate((own_table, got_table)):
            blocks = []
            for r in range(images):
                if group == 0:
                    block = x_ref[r, at, :]
                else:
                    block = got_ref[pl.ds(pl.multiple_of(r * rows + t * STEP, STEP), STEP), :]
                blocks.append(block.astype(jnp.float32))
            sums.append(
                [phase_sums(blocks, table, j, c) for j in range(len(outs)) for c in range(2)]
            )
        for m, (p, q) in enumerate(zip(*sums)):
            total = p.astype(jnp.float32) + q.astype(jnp.float32)
            outs[m // 2][m % 2, at, :] = total.astype(jnp.bfloat16)
        return carry

    lax.fori_loop(0, rows // STEP, body, 0)


def fit(table, x, got):
    _, rows, cols = x.shape
    out = jax.ShapeDtypeStruct((2, rows, cols), x.dtype)
    return pl.pallas_call(
        fit_kernel,
        out_shape=[out] * table.shape[0],
        in_specs=[VMEM] * 3,
        out_specs=[VMEM] * table.shape[0],
        scratch_shapes=[pltpu.VMEM(table.shape, table.dtype)],
        compiler_params=pltpu.CompilerParams(vmem_limit_bytes=16 * 1024 * 1024),
        name="fit",
    )(table, x, got)


def spread_kernel(x_ref, o_hbm, sems):
    me = lax.axis_index("x")
    count = o_hbm.shape[0]
    copies = [
        pltpu.make_async_copy(x_ref, o_hbm.at[jnp.bitwise_xor(me, i)], sems.at[i])
        for i in range(1, count)
    ]
    for copy in copies:
        copy.start()
    for copy in copies:
        copy.wait()


def spread(x, count):
    return pl.pallas_call(
        spread_kernel,
        out_shape=jax.ShapeDtypeStruct((count,) + x.shape, x.dtype),
        in_specs=[VMEM],
        out_specs=HBM,
        scratch_shapes=[pltpu.SemaphoreType.DMA((count,))],
        compiler_params=pltpu.CompilerParams(vmem_limit_bytes=16 * 1024 * 1024),
        name="spread",
    )(x)


def nt(a, b):
    return lax.dot_general(a, b, (((1,), (1,)), ((), ())), preferred_element_type=jnp.float32)


def join_kernel(*refs):
    out_ref = refs[-1]
    for j, ref in enumerate(refs[:-1]):
        out_ref[j] = ref[...]


def join(blocks):
    out = jax.ShapeDtypeStruct((len(blocks),) + blocks[0].shape, jnp.bfloat16)
    return pl.pallas_call(
        join_kernel,
        out_shape=out,
        in_specs=[VMEM] * len(blocks),
        out_specs=VMEM,
        compiler_params=pltpu.CompilerParams(vmem_limit_bytes=16 * 1024 * 1024),
        cost_estimate=pl.CostEstimate(
            flops=JOIN_COST, bytes_accessed=2 * out.size * 2, transcendentals=0
        ),
        name="join",
    )(*blocks)


def rows_kernel(first_ref, *refs):
    late, refs = refs[: len(LATE)], refs[len(LATE) :]
    own_ref, g_ref, w_ref, part_ref, dens, fit = refs
    xs, groups, pack, _ = g_ref.shape
    half = pack // 2
    kp = lax.axis_index("kp")
    width = first_ref.shape[3]
    blocks = [(j, first_ref.at[i]) for i, j in enumerate(EARLY)] + list(zip(LATE, late))
    for j, ref in blocks:
        at = pl.ds(pl.multiple_of(jnp.bitwise_xor(kp, j) * width, width), width)
        for c in range(2):
            fit[c, :, at] = ref[c]
    me = lax.axis_index("x")
    for g in range(groups):
        mine = own_ref[g]
        for x in range(0, xs, 2):
            first = jnp.where(me == x, mine, g_ref[x, g])
            second = jnp.where(me == x + 1, mine, g_ref[x + 1, g])
            at = pl.ds((g * xs + x) * half, pack)
            for c in range(2):
                cut = slice(c * half, (c + 1) * half)
                dens[c, at, :] = jnp.concatenate([first[cut], second[cut]], axis=0)
    f_real, f_imag = fit[0], fit[1]
    d_real, d_imag = dens[0], dens[1]
    w_real = (nt(f_real, d_real) - nt(f_imag, d_imag)).astype(jnp.bfloat16)
    w_ref[0] = w_real
    w_imag = (nt(f_real, d_imag) + nt(f_imag, d_real)).astype(jnp.bfloat16)
    w_ref[1] = w_imag
    n = f_real.shape[0]
    aux = n // ROWS
    row = lax.broadcasted_iota(jnp.int32, (n, n), 0)
    col = lax.broadcasted_iota(jnp.int32, (n, n), 1)
    same = jnp.bitwise_and(row, aux - 1) == jnp.bitwise_and(col, aux - 1)
    sums = []
    for gram in (
        nt(w_real, f_real) + nt(w_imag, f_imag),
        nt(w_imag, f_real) - nt(w_real, f_imag),
    ):
        kept = jnp.where(same, gram, 0.0)
        for i in range(ROWS):
            sums.append(jnp.sum(kept[i * aux : (i + 1) * aux], axis=0, keepdims=True))
    stacked = jnp.concatenate(sums, axis=0)
    count = 2 * ROWS
    lane = lax.broadcasted_iota(jnp.int32, (count, LANES), 1)
    sub = lax.broadcasted_iota(jnp.int32, (count, LANES), 0)
    terms = jnp.zeros((count, LANES), jnp.float32)
    at_col = lax.broadcasted_iota(jnp.int32, (count, n), 1)
    for j in range(ROWS):
        mine = jnp.logical_and(at_col >= j * aux, at_col < (j + 1) * aux)
        total = jnp.sum(jnp.where(mine, stacked, 0.0), axis=1, keepdims=True)
        terms = terms + jnp.where(lane == sub * ROWS + j, total, 0.0)
    part_ref[...] = jnp.sum(terms, axis=0, keepdims=True)


def exchange(first, late, own, g):
    _, _, rows, width = first.shape
    n = width * (len(EARLY) + len(LATE))
    wide = jax.ShapeDtypeStruct((2, rows, n), jnp.bfloat16)
    return pl.pallas_call(
        rows_kernel,
        out_shape=(wide, jax.ShapeDtypeStruct((1, LANES), jnp.float32)),
        in_specs=[VMEM] * (3 + len(LATE)),
        out_specs=(VMEM, VMEM),
        scratch_shapes=[
            pltpu.VMEM((2, n, n), jnp.bfloat16),
            pltpu.VMEM(wide.shape, wide.dtype),
        ],
        compiler_params=pltpu.CompilerParams(vmem_limit_bytes=32 * 1024 * 1024),
        name="exchange",
    )(first, *late, own, g)


def leave_kernel(w_ref, w_hbm, sems):
    copies = [pltpu.make_async_copy(w_ref.at[c], w_hbm.at[c], sems.at[c]) for c in range(2)]
    for copy in copies:
        copy.start()
    for copy in copies:
        copy.wait()


def leave(w):
    return pl.pallas_call(
        leave_kernel,
        out_shape=jax.ShapeDtypeStruct(w.shape, w.dtype),
        in_specs=[VMEM],
        out_specs=HBM,
        scratch_shapes=[pltpu.SemaphoreType.DMA((2,))],
        compiler_params=pltpu.CompilerParams(vmem_limit_bytes=16 * 1024 * 1024),
        cost_estimate=pl.CostEstimate(
            flops=JOIN_COST, bytes_accessed=4 * w.size, transcendentals=0
        ),
        name="leave",
    )(w)


def terms_over(part, axes):
    count = lax.axis_size(axes)
    block = jnp.broadcast_to(part[None], (count,) + part.shape)
    return lax.all_to_all(block, axes, 0, 0, tiled=True)


def on_device(lattice, kpoints, tensors, density):
    kp_count = lax.axis_size("kp")
    images, rows, aux_local, orb_local = tensors.shape
    n = orb_local * kp_count
    near, xs = lax.axis_size(("z", "ylo")), lax.axis_size("x")
    piece = density[0].transpose(0, 2, 1).reshape(-1, n)
    images_held = tensors.reshape(images, -1, orb_local)
    packed, block, table = pack(kpoints, lattice, images_held, piece, kp_count, near)
    got = lax.ppermute(packed, "img", [(0, 1), (1, 0)])
    own = lax.all_to_all(block, ("z", "ylo"), 0, 0, tiled=True)
    fitted = fit(table, images_held, got)
    fitted = [
        block if j == 0 else lax.ppermute(block, "kp", [(i, i ^ j) for i in range(kp_count)])
        for j, block in enumerate(fitted)
    ]
    dens = lax.all_to_all(spread(own, xs), "x", 0, 0, tiled=True)

    products, part = exchange(join([fitted[j] for j in EARLY]), [fitted[j] for j in LATE], own, dens)
    part = jnp.sum(terms_over(part, ("z", "img")), axis=0)
    part = jnp.sum(terms_over(part, ("x", "ylo", "kp")), axis=0)
    scale = 1.0 / math.sqrt(NK * NAUX * NAO)
    tile = part[0, : 2 * ROWS * ROWS].reshape(2, ROWS, ROWS) * scale
    return leave(products).reshape(1, 2, rows, aux_local, n), tile


def solution(mesh):
    fine = Mesh(mesh.devices.reshape(8, 2, 4, 4, 2), ("z", "ylo", "x", "kp", "img"))
    aux = ("z", "ylo", "x")
    return jax.shard_map(
        on_device,
        mesh=fine,
        in_specs=(
            P("img", None),
            P(),
            P("img", None, aux, "kp"),
            P(("kp", "img"), None, None, aux),
        ),
        out_specs=(P(("kp", "img"), None, None, aux, None), P()),
        check_vma=False,
    )
```
